128 devices in a mesh: img: 16 (over z, x), cam: 8 (over y, core).
Axes of the slice: x: 4, y: 4, z: 4, core: 2. Of those that a mesh axis runs over, the one named last changes fastest.
Arguments:
- jac_cam: float32 [49152, 8, 9, 128], P(('img', 'cam')), may hold values from -0.125 to 0.125
- jac_point: float32 [49152, 8, 3, 128], P(('img', 'cam')), may hold values from -0.5 to 0.5
- residual: float32 [49152, 8, 128], P(('img', 'cam')), may hold values from -6 to 6
- obs_count: int32 [49152], P(('img', 'cam')), may hold values from 2 to 8
- obs_camera: int32 [49152, 8], P(('img', 'cam')), may hold values from 0 to 4095
Outputs:
- cam_factor: float32 [45, 4096], P(None, 'cam')
- cam_step: float32 [9, 4096], P(None, 'cam')
- point_step: float32 [3, 49152], P(None, ('img', 'cam'))
The draws below stay inside these ranges and needn't reach their ends.
All inputs are finite; a program needn't handle non-finite values.
Results may differ from the reference program's by a relative error of at most 0.000076.
Values sent between devices are 32-bit elements; how exact they have to be, the bound alone decides.
A program may use at most 192 MiB of HBM per device.

```python
import math
import jax
import jax.numpy as jnp
import numpy as np
from jax import lax

PATCH = 128
CP = 9
K = 8
NC = 4096
LANDMARKS = 49152


def with_ends(result, own_key, smallest, top_value):
    index_at = [jax.random.randint(jax.random.fold_in(own_key, axis), (), 0, length) for axis, length in enumerate(result.shape)]
    longest = result.shape.index(max(result.shape))
    neighbour = index_at[:longest] + [(index_at[longest] + 1) % result.shape[longest]] + index_at[longest + 1:]
    return result.at[tuple(index_at)].set(smallest).at[tuple(neighbour)].set(top_value)


def shard_levels(stream_key, dims, shards, least, largest):
    loudness, own = 1.0, jax.random.fold_in(stream_key, 6)
    for position, blocks in shards:
        steps = jnp.exp(jax.random.uniform(jax.random.fold_in(own, position), (blocks,), jnp.float32, least / len(shards), largest / len(shards)))
        loudness = loudness * jnp.repeat(steps, dims[position] // blocks).reshape([-1 if axis == position else 1 for axis in range(len(dims))])
    return loudness


def cumulative_ranks(count, slope):
    portions = [(1 << 20) // math.isqrt(grade ** slope) + 1 for grade in range(1, count + 1)]
    spread = 1 + sum(portions) // (1 << 30)
    return np.cumsum(np.array([max(1, weight // spread) for weight in portions]))


def skewed_ids(key, shape, number_of, slope):
    listing = cumulative_ranks(number_of, slope)
    ticket = jax.random.randint(jax.random.fold_in(key, 1), shape, 0, int(listing[number_of - 1]))
    grade = jnp.searchsorted(jnp.asarray(listing, jnp.int32), ticket, side="right")
    return jax.random.permutation(jax.random.fold_in(key, 2), number_of)[grade].astype(jnp.int32)


def scatter_about(rng, extent, spread, reach, pieces=(), held_as=jnp.bfloat16):
    result = spread * jax.random.normal(rng, extent, jnp.float32)
    if pieces:
        result = result * shard_levels(rng, extent, pieces, -0.22, 0.18)
    return jnp.clip(result, -reach, reach).astype(held_as)


def setup_inputs(seed: int = 0) -> dict:
    keys = jax.random.split(jax.random.key(seed), 6)
    return {
        "jac_cam": scatter_about(keys[0], (LANDMARKS, K, CP, PATCH), (PATCH * 16) ** -0.5, 0.125, ((0, 128),), jnp.float32),
        "jac_point": scatter_about(keys[1], (LANDMARKS, K, 3, PATCH), PATCH ** -0.5, 0.5, ((0, 128),), jnp.float32),
        "residual": scatter_about(keys[2], (LANDMARKS, K, PATCH), 1.0, 6.0, ((0, 128),), jnp.float32),
        "obs_count": with_ends(jax.random.randint(keys[3], (LANDMARKS,), 2, K + 1), jax.random.fold_in(keys[3], 1), 2, K).astype(jnp.int32),
        "obs_camera": with_ends(skewed_ids(keys[4], (LANDMARKS, K), NC, 1), jax.random.fold_in(keys[4], 3), 0, NC - 1).astype(jnp.int32),
    }


highest = lax.Precision.HIGHEST
lm_lambda = 0.5

def marginalize(jac_cam, jac_point, residual, obs_count):
    slot_count = jac_cam.shape[1]
    live_mask = (jnp.arange(slot_count, dtype=jnp.int32)[None, :] < obs_count[:, None]).astype(jac_cam.dtype)
    cam_rows = jac_cam * live_mask[:, :, None, None]
    point_rows = jac_point * live_mask[:, :, None, None]
    res_rows = residual * live_mask[:, :, None]

    def inner_product(left, right):
        return lax.optimization_barrier(jnp.sum(left * right, axis=(1, 2)))
    column_zero = point_rows[:, :, 0, :]
    column_one = point_rows[:, :, 1, :]
    column_two = point_rows[:, :, 2, :]
    norm_zero = jnp.sqrt(inner_product(column_zero, column_zero))
    basis_zero = column_zero / norm_zero[:, None, None]
    upper_zero_one = inner_product(basis_zero, column_one)
    remain_one = column_one - upper_zero_one[:, None, None] * basis_zero
    norm_one = jnp.sqrt(inner_product(remain_one, remain_one))
    basis_one = remain_one / norm_one[:, None, None]
    upper_zero_two = inner_product(basis_zero, column_two)
    upper_one_two = inner_product(basis_one, column_two)
    remain_two = column_two - upper_zero_two[:, None, None] * basis_zero - upper_one_two[:, None, None] * basis_one
    norm_two = jnp.sqrt(inner_product(remain_two, remain_two))
    basis_two = remain_two / norm_two[:, None, None]
    basis_rows = jnp.stack([basis_zero, basis_one, basis_two], axis=2)
    coupling = jnp.einsum('lkpx,lkcx->lkpc', basis_rows, cam_rows, precision=highest)
    reduced_rhs = jnp.einsum('lkpx,lkx->lp', basis_rows, res_rows, precision=highest)
    obs_gram = jnp.einsum('lkcx,lkdx->lkcd', cam_rows, cam_rows, precision=highest) - jnp.einsum('lkpc,lkpd->lkcd', coupling, coupling, precision=highest)
    obs_grad = jnp.einsum('lkcx,lkx->lkc', cam_rows, res_rows, precision=highest) - jnp.einsum('lkpc,lp->lkc', coupling, reduced_rhs, precision=highest)
    point_factor = (norm_zero, upper_zero_one, upper_zero_two, norm_one, upper_one_two, norm_two)
    return (obs_gram, obs_grad, coupling, reduced_rhs, point_factor)

def point_update(coupling, reduced_rhs, point_factor, camera_table, obs_camera):
    picked = camera_table[obs_camera]
    totals = reduced_rhs + jnp.einsum('lkpc,lkc->lp', coupling, picked, precision=highest)
    norm_zero, upper_zero_one, upper_zero_two, norm_one, upper_one_two, norm_two = point_factor
    solved_two = totals[:, 2] / norm_two
    solved_one = (totals[:, 1] - upper_one_two * solved_two) / norm_one
    solved_zero = (totals[:, 0] - upper_zero_one * solved_one - upper_zero_two * solved_two) / norm_zero
    return -jnp.stack([solved_zero, solved_one, solved_two], axis=0)

def reference(jac_cam, jac_point, residual, obs_count, obs_camera):
    obs_gram, obs_grad, coupling, reduced_rhs, point_factor = marginalize(jac_cam, jac_point, residual, obs_count)
    camera_ids = obs_camera.reshape(-1)
    block_gram = jax.ops.segment_sum(obs_gram.reshape(-1, CP, CP), camera_ids, num_segments=NC)
    block_grad = jax.ops.segment_sum(obs_grad.reshape(-1, CP), camera_ids, num_segments=NC)
    damped = block_gram + lm_lambda * jnp.eye(CP, dtype=block_gram.dtype)[None, :, :]
    lower = jnp.linalg.cholesky(damped)
    upper = jnp.swapaxes(lower, 1, 2)
    cam_factor = jnp.stack([upper[:, i, j] for i in range(CP) for j in range(i, CP)], axis=0)
    forward = []
    for j in range(CP):
        amount = block_grad[:, j]
        for k in range(j):
            amount = amount - upper[:, k, j] * forward[k]
        forward.append(amount / upper[:, j, j])
    backward = [None] * CP
    for i in range(CP - 1, -1, -1):
        amount = forward[i]
        for j in range(i + 1, CP):
            amount = amount - upper[:, i, j] * backward[j]
        backward[i] = amount / upper[:, i, i]
    cam_step = -jnp.stack(backward, axis=0)
    point_step = point_update(coupling, reduced_rhs, point_factor, jnp.transpose(cam_step), obs_camera)
    return (cam_factor, cam_step, point_step)
```

```python
import functools

import jax
import jax.numpy as jnp
from jax import lax
from jax.experimental import pallas as pl
from jax.experimental.pallas import tpu as pltpu
from jax.sharding import PartitionSpec as P

CP = 9
K = 8
NL = 384
NB = 3
NOBS = NL * K
PACKED = 45
ROWS = 56
NIMG = 16
NY = 4
LM_LAMBDA = 0.5
f32 = jnp.float32
bf16 = jnp.bfloat16
MESH = pl.DeviceIdType.MESH

CC = [(i, j) for i in range(CP) for j in range(i, CP)]
CR = [(i, 9) for i in range(CP)]
QC = [(10 + p, c) for p in range(3) for c in range(CP)]
QR = [(10 + p, 9) for p in range(3)]
PAIRS = CC + CR + QC + QR
GROUPS = [PAIRS[0:28], PAIRS[28:56], PAIRS[56:84]]


def marginalize_kernel(
    jc, jp, rs, cnt, cam, rec_out, coup_out, small_out, cam_out,
    jcv, jpv, rsv, qt, ta, tb, acc, rec, sem,
):
    def copy(b, which):
        s = pl.ds(b * 128, 128)
        src, dst = ((jp, jpv), (jc, jcv), (rs, rsv))[which]
        return pltpu.make_async_copy(src.at[s], dst.at[s], sem.at[b, which])

    for which in range(3):
        for b in range(NB):
            copy(b, which).start()

    jcf = jcv.reshape(NL * CP * K, 128)
    jpf = jpv.reshape(NL * 3 * K, 128)
    rsf = rsv.reshape(NL * K, 128)

    for b in range(NB):
        for k in range(K):
            cam_out[0:1, (b * K + k) * 128 : (b * K + k + 1) * 128] = cam[k : k + 1, b * 128 : (b + 1) * 128]

    def point_phase(b, _):
        copy(b, 0).wait()
        count = cnt[pl.ds(b, 1), :]
        zero = jnp.zeros((8, 128), f32)

        def first(k, sums):
            live = (count > k).astype(f32)
            parts = []
            for p in range(3):
                v = jpf[pl.ds(b * (128 * 3 * K) + p * K + k, 128, stride=3 * K), :].T * live
                qt[p, b * K + k] = v
                parts.append(v)
            sums = list(sums)
            for x in range(16):
                a = [v[8 * x : 8 * x + 8] for v in parts]
                for q in range(3):
                    sums[q] = sums[q] + a[0] * a[q]
            return tuple(sums)

        s00, s01, s02 = [
            jnp.sum(v, axis=0, keepdims=True) for v in lax.fori_loop(0, K, first, (zero,) * 3)
        ]
        norm0 = jnp.sqrt(s00)
        inv0 = 1.0 / norm0
        r01 = s01 * inv0
        r02 = s02 * inv0
        c01 = r01 * inv0
        c02 = r02 * inv0

        def second(k, sums):
            n1, s12 = sums
            for x in range(16):
                rows = pl.ds(8 * x, 8)
                rem = qt[1, b * K + k, rows, :] - c01 * qt[0, b * K + k, rows, :]
                qt[1, b * K + k, rows, :] = rem
                n1 = n1 + rem * rem
                s12 = s12 + rem * qt[2, b * K + k, rows, :]
            return n1, s12

        n11, s12 = [
            jnp.sum(v, axis=0, keepdims=True) for v in lax.fori_loop(0, K, second, (zero,) * 2)
        ]
        norm1 = jnp.sqrt(n11)
        inv1 = 1.0 / norm1
        r12 = s12 * inv1
        c12 = r12 * inv1

        def third(k, n2):
            for x in range(16):
                rows = pl.ds(8 * x, 8)
                rem = (
                    qt[2, b * K + k, rows, :]
                    - c02 * qt[0, b * K + k, rows, :]
                    - c12 * qt[1, b * K + k, rows, :]
                )
                qt[2, b * K + k, rows, :] = rem
                n2 = n2 + rem * rem
            return n2

        n22 = jnp.sum(lax.fori_loop(0, K, third, zero), axis=0, keepdims=True)
        norm2 = jnp.sqrt(n22)
        inv2 = 1.0 / norm2
        for n, v in enumerate((inv0, inv1, inv2, r01, r02, r12)):
            small_out[b, n : n + 1, :] = v
        return 0

    lax.fori_loop(0, NB, point_phase, 0)

    def turn(b, k, t):
        for c in range(CP):
            t[c] = jcf[pl.ds(b * (128 * CP * K) + c * K + k, 128, stride=CP * K), :].T
        t[9] = rsf[pl.ds(b * (128 * K) + k, 128, stride=K), :].T

    def products(b, k, t):
        base = 0
        for pairs in GROUPS:
            total = [None] * len(pairs)
            for x in range(16):
                rows = pl.ds(8 * x, 8)
                held = {}
                for n, pair in enumerate(pairs):
                    for q in pair:
                        if q not in held:
                            held[q] = t[q, rows, :] if q < 10 else qt[q - 10, b * K + k, rows, :]
                    term = held[pair[0]] * held[pair[1]]
                    total[n] = term if total[n] is None else total[n] + term
            for n in range(len(pairs)):
                acc[base + n, pl.ds(pl.multiple_of(k * 8, 8), 8), :] = total[n]
            base += len(pairs)

    def camera_phase(b, _):
        copy(b, 1).wait()
        copy(b, 2).wait()
        turn(b, 0, ta)

        def two(h, _):
            turn(b, 2 * h + 1, tb)
            products(b, 2 * h, ta)
            turn(b, jnp.minimum(2 * h + 2, K - 1), ta)
            products(b, 2 * h + 1, tb)
            return 0

        lax.fori_loop(0, K // 2, two, 0)

        def entry(n):
            v = acc[n, pl.ds(0, 8, stride=8), :]
            for s in range(1, 8):
                v = v + acc[n, pl.ds(s, 8, stride=8), :]
            return v

        slot = lax.broadcasted_iota(jnp.int32, (8, 128), 0)
        live = (slot < cnt[pl.ds(b, 1), :]).astype(f32)
        inv = [small_out[b, p : p + 1, :] for p in range(3)]
        coupling = [[entry(54 + p * CP + c) * inv[p] for c in range(CP)] for p in range(3)]
        for p in range(3):
            for c in range(CP):
                coup_out[b, p * CP + c] = coupling[p][c]
        rhs = [jnp.sum(entry(81 + p), axis=0, keepdims=True) * inv[p] for p in range(3)]
        for p in range(3):
            small_out[b, 6 + p : 7 + p, :] = rhs[p]
        for n, (i, j) in enumerate(CC):
            v = entry(n) * live
            for p in range(3):
                v = v - coupling[p][i] * coupling[p][j]
            rec[n * 8 : n * 8 + 8, :] = v
        for i in range(CP):
            v = entry(45 + i) * live
            for p in range(3):
                v = v - coupling[p][i] * rhs[p]
            rec[(45 + i) * 8 : (45 + i) * 8 + 8, :] = v
        for i in range(54, ROWS):
            rec[i * 8 : i * 8 + 8, :] = jnp.zeros((8, 128), f32)
        for k in range(K):
            v = rec[pl.ds(k, ROWS, stride=8), :]
            high = v.astype(bf16).astype(f32)
            both = jnp.concatenate([high, v - high], axis=0).astype(bf16)
            rec_out[:, pl.ds(pl.multiple_of((b * K + k) * 128, 128), 128)] = both
        return 0

    lax.fori_loop(0, NB, camera_phase, 0)


def marginalize(jac_cam, jac_point, residual, count, cam):
    hbm = pl.BlockSpec(memory_space=pltpu.MemorySpace.HBM)
    vmem = pl.BlockSpec(memory_space=pltpu.MemorySpace.VMEM)
    return pl.pallas_call(
        marginalize_kernel,
        out_shape=(
            jax.ShapeDtypeStruct((2 * ROWS, NOBS), bf16),
            jax.ShapeDtypeStruct((NB, 27, 8, 128), f32),
            jax.ShapeDtypeStruct((NB, 16, 128), f32),
            jax.ShapeDtypeStruct((1, NOBS), jnp.int32),
        ),
        in_specs=[hbm, hbm, hbm, vmem, vmem],
        out_specs=(vmem,) * 4,
        scratch_shapes=[
            pltpu.VMEM((NL, CP, K, 128), f32),
            pltpu.VMEM((NL, 3, K, 128), f32),
            pltpu.VMEM((NL, K, 128), f32),
            pltpu.VMEM((3, NB * K, 128, 128), f32),
            pltpu.VMEM((10, 128, 128), f32),
            pltpu.VMEM((10, 128, 128), f32),
            pltpu.VMEM((len(PAIRS), 64, 128), f32),
            pltpu.VMEM((ROWS * 8, 128), f32),
            pltpu.SemaphoreType.DMA((NB, 3)),
        ],
        compiler_params=pltpu.CompilerParams(vmem_limit_bytes=52 << 20),
        cost_estimate=pl.CostEstimate(flops=70_000_000, bytes_accessed=21_000_000, transcendentals=0),
        name="marginalize",
    )(jac_cam, jac_point, residual, count, cam)


def pair_positions():
    position = {}
    for i in range(CP):
        for j in range(i, CP):
            position[i, j] = len(position)
    return position


def camera_solve(load):
    position = pair_positions()
    factor, inverse = {}, []
    for j in range(CP):
        for i in range(j, CP):
            amount = load(position[j, i])
            if i == j:
                amount = amount + LM_LAMBDA
            for k in range(j):
                amount = amount - factor[k, j] * factor[k, i]
            if i == j:
                factor[j, j] = jnp.sqrt(amount)
                inverse.append(1.0 / factor[j, j])
            else:
                factor[j, i] = amount * inverse[j]
    forward = []
    for j in range(CP):
        amount = load(PACKED + j)
        for k in range(j):
            amount = amount - factor[k, j] * forward[k]
        forward.append(amount * inverse[j])
    backward = [None] * CP
    for i in range(CP - 1, -1, -1):
        amount = forward[i]
        for j in range(i + 1, CP):
            amount = amount - factor[i, j] * backward[j]
        backward[i] = amount * inverse[i]
    return [factor[i, j] for i in range(CP) for j in range(i, CP)], [-v for v in backward]


def fill_onehot(cam, onehot):
    for t in range(NOBS // 256):
        lane = cam[0:1, t * 256 : (t + 1) * 256] & 255
        hit = lax.broadcasted_iota(jnp.int32, (256, 256), 0) == lane
        onehot[:, t * 256 : (t + 1) * 256] = hit.astype(f32).astype(bf16)


def camera_kernel(
    rec, cam, fac_out, steps,
    onehot, lhs, away, home, from_core, from_y, block, from_img, full, spread,
    send_a, recv_a, send_b, recv_b, send_c, recv_c, send_d, recv_d, send_e, recv_e,
):
    img, mine = lax.axis_index("img"), lax.axis_index("cam")
    y, core = mine // 2, mine % 2

    barrier = pltpu.get_barrier_semaphore()
    for d in range(1, NIMG):
        pl.semaphore_signal(barrier, inc=1, device_id=((img + d) % NIMG, mine), device_id_type=MESH)
    for d in range(1, 8):
        pl.semaphore_signal(barrier, inc=1, device_id=(img, (mine + d) % 8), device_id_type=MESH)

    fill_onehot(cam, onehot)

    def sums_of(owner):
        for half in range(2):
            for t in range(6):
                cols = slice(t * 512, (t + 1) * 512)
                hit = (cam[0:1, cols] >> 8) == owner * 2 + half
                mask = jnp.broadcast_to(hit.astype(f32), (16, 512)).astype(bf16)
                mask = jnp.concatenate([mask] * 7, axis=0)
                lhs[half * 112 : (half + 1) * 112, cols] = rec[:, cols] * mask
        r = lax.dot_general(
            lhs[...], onehot[...], (((1,), (1,)), ((), ())), preferred_element_type=f32
        )
        return [r[112 * h : 112 * h + 56] + r[112 * h + 56 : 112 * h + 112] for h in range(2)]

    to_core = []
    for d in range(4):
        to_y = (y + 2 - d + 4) % 4
        sums = sums_of(to_y * 2 + 1 - core)
        for h in range(2):
            away[d, h] = sums[h]
        if d == 0:
            pl.semaphore_wait(barrier, 22)
        copy = pltpu.make_async_remote_copy(
            src_ref=away.at[d], dst_ref=from_core.at[d], send_sem=send_a.at[d], recv_sem=recv_a.at[d],
            device_id=(img, y * 2 + 1 - core), device_id_type=MESH,
        )
        copy.start()
        to_core.append(copy)

    to_ys = []
    for d in range(4):
        away_by = (2 - d + 4) % 4
        to_y = (y + away_by) % 4
        sums = sums_of(to_y * 2 + core)
        to_core[d].wait_recv()
        for h in range(2):
            home[d, h] = sums[h] + from_core[d, h]
        if away_by:
            copy = pltpu.make_async_remote_copy(
                src_ref=home.at[d], dst_ref=from_y.at[away_by - 1],
                send_sem=send_b.at[away_by - 1], recv_sem=recv_b.at[away_by - 1],
                device_id=(img, to_y * 2 + core), device_id_type=MESH,
            )
            copy.start()
            to_ys.append(copy)
    own = 2
    for copy in to_ys:
        copy.wait_recv()
    for h in range(2):
        total = home[own, h] + from_y[0, h] + from_y[1, h] + from_y[2, h]
        for r in range(7):
            block[h * 7 + r] = total[8 * r : 8 * r + 8]

    def slice_copy(d):
        return pltpu.make_async_remote_copy(
            src_ref=block.at[(img + d) % NIMG], dst_ref=from_img.at[d],
            send_sem=send_c.at[d], recv_sem=recv_c.at[d],
            device_id=((img + d) % NIMG, mine), device_id_type=MESH,
        )

    for d in range(1, NIMG):
        @pl.when((img + d) % NIMG < 14)
        def _(d=d):
            slice_copy(d).start()

    def sum_copy(d):
        return pltpu.make_async_remote_copy(
            src_ref=full.at[img], dst_ref=full.at[img],
            send_sem=send_d.at[d], recv_sem=recv_d.at[d],
            device_id=((img + d) % NIMG, mine), device_id_type=MESH,
        )

    @pl.when(img < 14)
    def _():
        for d in range(1, NIMG):
            slice_copy(d).wait_recv()
        total = block[img]
        for d in range(1, NIMG):
            total = total + from_img[d]
        full[img] = total
        for d in range(1, NIMG):
            sum_copy(d).start()

    for d in range(1, NIMG):
        @pl.when((img - d + NIMG) % NIMG < 14)
        def _(d=d):
            sum_copy(d).wait_recv()

    for h in range(2):
        for r in range(7):
            for e in range(2):
                spread[pl.ds(r * 32 + h * 2 + e, 8, stride=4), :] = full[h * 7 + r, :, e * 128 : (e + 1) * 128]
    factor, step = camera_solve(lambda c: spread[4 * c : 4 * c + 4, :])
    for n, v in enumerate(factor):
        for q in range(4):
            fac_out[n : n + 1, q * 128 : (q + 1) * 128] = v[q : q + 1]
    steps[mine] = jnp.zeros((2, 16, 256), f32)
    for n, v in enumerate(step):
        for q in range(4):
            steps[mine, q // 2, n : n + 1, (q % 2) * 128 : (q % 2 + 1) * 128] = v[q : q + 1]

    to_cams = []
    for d in range(1, 8):
        copy = pltpu.make_async_remote_copy(
            src_ref=steps.at[mine], dst_ref=steps.at[mine],
            send_sem=send_e.at[d], recv_sem=recv_e.at[d],
            device_id=(img, (mine + d) % 8), device_id_type=MESH,
        )
        copy.start()
        to_cams.append(copy)

    for copy in to_core + to_ys:
        copy.wait_send()
    for d in range(1, NIMG):
        @pl.when((img + d) % NIMG < 14)
        def _(d=d):
            slice_copy(d).wait_send()

    @pl.when(img < 14)
    def _():
        for d in range(1, NIMG):
            sum_copy(d).wait_send()

    for copy in to_cams:
        copy.wait_recv()
    for copy in to_cams:
        copy.wait_send()


def camera_update(records, cam):
    vmem = pl.BlockSpec(memory_space=pltpu.MemorySpace.VMEM)
    dma = pltpu.SemaphoreType.DMA
    return pl.pallas_call(
        camera_kernel,
        out_shape=(
            jax.ShapeDtypeStruct((PACKED, 512), f32),
            jax.ShapeDtypeStruct((8, 2, 16, 256), f32),
        ),
        in_specs=[vmem, vmem],
        out_specs=(vmem, vmem),
        scratch_shapes=[
            pltpu.VMEM((256, NOBS), bf16),
            pltpu.VMEM((224, NOBS), bf16),
            pltpu.VMEM((4, 2, ROWS, 256), f32),
            pltpu.VMEM((4, 2, ROWS, 256), f32),
            pltpu.VMEM((4, 2, ROWS, 256), f32),
            pltpu.VMEM((3, 2, ROWS, 256), f32),
            pltpu.VMEM((NIMG, 8, 256), f32),
            pltpu.VMEM((NIMG, 8, 256), f32),
            pltpu.VMEM((NIMG, 8, 256), f32),
            pltpu.VMEM((ROWS * 4, 128), f32),
            dma((4,)), dma((4,)), dma((3,)), dma((3,)), dma((NIMG,)), dma((NIMG,)),
            dma((NIMG,)), dma((NIMG,)), dma((8,)), dma((8,)),
        ],
        compiler_params=pltpu.CompilerParams(
            collective_id=0, has_side_effects=True, vmem_limit_bytes=40 << 20
        ),
        name="camera_update",
    )(records, cam)


def point_kernel(fac, steps, cam, coup, small, fac_out, step_out, point_out, onehot, picked):
    mine = lax.axis_index("cam")
    fac_out[...] = fac[...]
    for h in range(2):
        step_out[:, h * 256 : (h + 1) * 256] = steps[mine, h, 0:CP, :]
    fill_onehot(cam, onehot)
    table = steps[...].reshape(256, 256)
    high = table.astype(bf16)
    low = (table - high.astype(f32)).astype(bf16)
    for b in range(NB):
        for q in range(4):
            cols = slice(b * 1024 + q * 256, b * 1024 + (q + 1) * 256)
            chosen = jnp.dot(high, onehot[:, cols], preferred_element_type=f32) + jnp.dot(
                low, onehot[:, cols], preferred_element_type=f32
            )
            group = cam[0:1, cols] >> 8
            total = jnp.zeros((16, 256), f32)
            for g in range(16):
                total = total + jnp.where(group == g, chosen[16 * g : 16 * g + 16], 0.0)
            for e in range(2):
                picked[pl.ds(q * 2 + e, 16, stride=8), :] = total[:, e * 128 : (e + 1) * 128]
        sums = []
        for p in range(3):
            v = coup[b, p * CP] * picked[0:8, :]
            for c in range(1, CP):
                v = v + coup[b, p * CP + c] * picked[c * 8 : c * 8 + 8, :]
            sums.append(small[b, 6 + p : 7 + p, :] + jnp.sum(v, axis=0, keepdims=True))
        inv = [small[b, p : p + 1, :] for p in range(3)]
        r01, r02, r12 = [small[b, p : p + 1, :] for p in range(3, 6)]
        two = sums[2] * inv[2]
        one = (sums[1] - r12 * two) * inv[1]
        zero = (sums[0] - r01 * one - r02 * two) * inv[0]
        for p, v in enumerate((zero, one, two)):
            point_out[p : p + 1, b * 128 : (b + 1) * 128] = -v


def point_update(fac, steps, cam, coup, small):
    vmem = pl.BlockSpec(memory_space=pltpu.MemorySpace.VMEM)
    return pl.pallas_call(
        point_kernel,
        out_shape=(
            jax.ShapeDtypeStruct((PACKED, 512), f32),
            jax.ShapeDtypeStruct((CP, 512), f32),
            jax.ShapeDtypeStruct((3, NL), f32),
        ),
        in_specs=[vmem] * 5,
        out_specs=(vmem,) * 3,
        scratch_shapes=[pltpu.VMEM((256, NOBS), bf16), pltpu.VMEM((128, 128), f32)],
        compiler_params=pltpu.CompilerParams(vmem_limit_bytes=32 << 20),
        name="point_update",
    )(fac, steps, cam, coup, small)


def local(jac_cam, jac_point, residual, obs_count, obs_camera):
    records, coup, small, cam = marginalize(
        jnp.transpose(jac_cam, (0, 2, 1, 3)),
        jnp.transpose(jac_point, (0, 2, 1, 3)),
        residual,
        obs_count.reshape(NB, 128),
        jnp.transpose(obs_camera),
    )
    fac, steps = camera_update(records, cam)
    return point_update(fac, steps, cam, coup, small)


def solution(mesh):
    in_specs = (
        P(("img", "cam"), None, None, None),
        P(("img", "cam"), None, None, None),
        P(("img", "cam"), None, None),
        P(("img", "cam")),
        P(("img", "cam"), None),
    )
    out_specs = (P(None, "cam"), P(None, "cam"), P(None, ("img", "cam")))
    return jax.shard_map(local, mesh=mesh, in_specs=in_specs, out_specs=out_specs, check_vma=False)
```

```python
import functools

import jax
import jax.numpy as jnp
from jax import lax
from jax.experimental import pallas as pl
from jax.experimental.pallas import tpu as pltpu
from jax.sharding import PartitionSpec as P

CP = 9
K = 8
NL = 384
NB = 3
NOBS = NL * K
PACKED = 45
ROWS = 56
NIMG = 16
LM_LAMBDA = 0.5
f32 = jnp.float32
bf16 = jnp.bfloat16
MESH = pl.DeviceIdType.MESH

CC = [(i, j) for i in range(CP) for j in range(i, CP)]
CR = [(i, 9) for i in range(CP)]
QC = [(10 + p, c) for p in range(3) for c in range(CP)]
QR = [(10 + p, 9) for p in range(3)]
PAIRS = CC + CR + QC + QR
GROUPS = [PAIRS[0:28], PAIRS[28:56], PAIRS[56:84]]


def marginalize_kernel(
    jc, jp, rs, cnt_hbm, cam_hbm, rec_out, coup_out, small_out, cam_out,
    jcv, jpv, rsv, qt, ta, tb, acc, rec, cnt, cam, sem,
):
    def copy(b, which):
        s = pl.ds(b * 128, 128)
        src, dst = ((jp, jpv), (jc, jcv), (rs, rsv))[which]
        return pltpu.make_async_copy(src.at[s], dst.at[s], sem.at[b, which])

    count_copy = pltpu.make_async_copy(cnt_hbm, cnt, sem.at[NB, 0])
    cam_copy = pltpu.make_async_copy(cam_hbm, cam, sem.at[NB, 1])
    count_copy.start()
    for which in range(3):
        for b in range(NB):
            copy(b, which).start()
        if which == 0:
            cam_copy.start()
    count_copy.wait()

    jcf = jcv.reshape(NL * CP * K, 128)
    jpf = jpv.reshape(NL * 3 * K, 128)
    rsf = rsv.reshape(NL * K, 128)

    def point_phase(b, _):
        copy(b, 0).wait()
        count = cnt[pl.ds(b, 1), :]
        zero = jnp.zeros((8, 128), f32)

        def first(k, sums):
            live = (count > k).astype(f32)
            parts = []
            for p in range(3):
                v = jpf[pl.ds(b * (128 * 3 * K) + p * K + k, 128, stride=3 * K), :].T * live
                qt[p, b * K + k] = v
                parts.append(v)
            sums = list(sums)
            for x in range(16):
                a = [v[8 * x : 8 * x + 8] for v in parts]
                for q in range(3):
                    sums[q] = sums[q] + a[0] * a[q]
            return tuple(sums)

        s00, s01, s02 = [
            jnp.sum(v, axis=0, keepdims=True) for v in lax.fori_loop(0, K, first, (zero,) * 3)
        ]
        norm0 = jnp.sqrt(s00)
        inv0 = 1.0 / norm0
        r01 = s01 * inv0
        r02 = s02 * inv0
        c01 = r01 * inv0
        c02 = r02 * inv0

        def second(k, sums):
            n1, s12 = sums
            for x in range(16):
                rows = pl.ds(8 * x, 8)
                rem = qt[1, b * K + k, rows, :] - c01 * qt[0, b * K + k, rows, :]
                qt[1, b * K + k, rows, :] = rem
                n1 = n1 + rem * rem
                s12 = s12 + rem * qt[2, b * K + k, rows, :]
            return n1, s12

        n11, s12 = [
            jnp.sum(v, axis=0, keepdims=True) for v in lax.fori_loop(0, K, second, (zero,) * 2)
        ]
        norm1 = jnp.sqrt(n11)
        inv1 = 1.0 / norm1
        r12 = s12 * inv1
        c12 = r12 * inv1

        def third(k, n2):
            for x in range(16):
                rows = pl.ds(8 * x, 8)
                rem = (
                    qt[2, b * K + k, rows, :]
                    - c02 * qt[0, b * K + k, rows, :]
                    - c12 * qt[1, b * K + k, rows, :]
                )
                qt[2, b * K + k, rows, :] = rem
                n2 = n2 + rem * rem
            return n2

        n22 = jnp.sum(lax.fori_loop(0, K, third, zero), axis=0, keepdims=True)
        norm2 = jnp.sqrt(n22)
        inv2 = 1.0 / norm2
        for n, v in enumerate((inv0, inv1, inv2, r01, r02, r12)):
            small_out[b, n : n + 1, :] = v
        return 0

    lax.fori_loop(0, NB, point_phase, 0)

    def turn(b, k, t):
        for c in range(CP):
            t[c] = jcf[pl.ds(b * (128 * CP * K) + c * K + k, 128, stride=CP * K), :].T
        t[9] = rsf[pl.ds(b * (128 * K) + k, 128, stride=K), :].T

    def products(b, k, t):
        base = 0
        for pairs in GROUPS:
            total = [None] * len(pairs)
            for x in range(16):
                rows = pl.ds(8 * x, 8)
                held = {}
                for n, pair in enumerate(pairs):
                    for q in pair:
                        if q not in held:
                            held[q] = t[q, rows, :] if q < 10 else qt[q - 10, b * K + k, rows, :]
                    term = held[pair[0]] * held[pair[1]]
                    total[n] = term if total[n] is None else total[n] + term
            for n in range(len(pairs)):
                acc[base + n, pl.ds(pl.multiple_of(k * 8, 8), 8), :] = total[n]
            base += len(pairs)

    def camera_phase(b, _):
        copy(b, 1).wait()
        copy(b, 2).wait()
        turn(b, 0, ta)

        def two(h, _):
            turn(b, 2 * h + 1, tb)
            products(b, 2 * h, ta)
            turn(b, jnp.minimum(2 * h + 2, K - 1), ta)
            products(b, 2 * h + 1, tb)
            return 0

        lax.fori_loop(0, K // 2, two, 0)

        def entry(n):
            v = acc[n, pl.ds(0, 8, stride=8), :]
            for s in range(1, 8):
                v = v + acc[n, pl.ds(s, 8, stride=8), :]
            return v

        slot = lax.broadcasted_iota(jnp.int32, (8, 128), 0)
        live = (slot < cnt[pl.ds(b, 1), :]).astype(f32)
        inv = [small_out[b, p : p + 1, :] for p in range(3)]
        coupling = [[entry(54 + p * CP + c) * inv[p] for c in range(CP)] for p in range(3)]
        for p in range(3):
            for c in range(CP):
                coup_out[b, p * CP + c] = coupling[p][c]
        rhs = [jnp.sum(entry(81 + p), axis=0, keepdims=True) * inv[p] for p in range(3)]
        for p in range(3):
            small_out[b, 6 + p : 7 + p, :] = rhs[p]
        for n, (i, j) in enumerate(CC):
            v = entry(n) * live
            for p in range(3):
                v = v - coupling[p][i] * coupling[p][j]
            rec[n * 8 : n * 8 + 8, :] = v
        for i in range(CP):
            v = entry(45 + i) * live
            for p in range(3):
                v = v - coupling[p][i] * rhs[p]
            rec[(45 + i) * 8 : (45 + i) * 8 + 8, :] = v
        for i in range(54, ROWS):
            rec[i * 8 : i * 8 + 8, :] = jnp.zeros((8, 128), f32)
        for k in range(K):
            v = rec[pl.ds(k, ROWS, stride=8), :]
            high = v.astype(bf16).astype(f32)
            both = jnp.concatenate([high, v - high], axis=0).astype(bf16)
            rec_out[:, pl.ds(pl.multiple_of((b * K + k) * 128, 128), 128)] = both
        return 0

    lax.fori_loop(0, NB, camera_phase, 0)
    cam_copy.wait()
    for b in range(NB):
        for k in range(K):
            cam_out[0:1, (b * K + k) * 128 : (b * K + k + 1) * 128] = cam[k : k + 1, b * 128 : (b + 1) * 128]


def marginalize(jac_cam, jac_point, residual, count, cam):
    hbm = pl.BlockSpec(memory_space=pltpu.MemorySpace.HBM)
    vmem = pl.BlockSpec(memory_space=pltpu.MemorySpace.VMEM)
    return pl.pallas_call(
        marginalize_kernel,
        out_shape=(
            jax.ShapeDtypeStruct((2 * ROWS, NOBS), bf16),
            jax.ShapeDtypeStruct((NB, 27, 8, 128), f32),
            jax.ShapeDtypeStruct((NB, 16, 128), f32),
            jax.ShapeDtypeStruct((1, NOBS), jnp.int32),
        ),
        in_specs=[hbm] * 5,
        out_specs=(vmem,) * 4,
        scratch_shapes=[
            pltpu.VMEM((NL, CP, K, 128), f32),
            pltpu.VMEM((NL, 3, K, 128), f32),
            pltpu.VMEM((NL, K, 128), f32),
            pltpu.VMEM((3, NB * K, 128, 128), f32),
            pltpu.VMEM((10, 128, 128), f32),
            pltpu.VMEM((10, 128, 128), f32),
            pltpu.VMEM((len(PAIRS), 64, 128), f32),
            pltpu.VMEM((ROWS * 8, 128), f32),
            pltpu.VMEM((NB, 128), jnp.int32),
            pltpu.VMEM((K, NL), jnp.int32),
            pltpu.SemaphoreType.DMA((NB + 1, 3)),
        ],
        compiler_params=pltpu.CompilerParams(vmem_limit_bytes=52 << 20),
        cost_estimate=pl.CostEstimate(flops=70_000_000, bytes_accessed=21_000_000, transcendentals=0),
        name="marginalize",
    )(jac_cam, jac_point, residual, count, cam)


def pair_positions():
    position = {}
    for i in range(CP):
        for j in range(i, CP):
            position[i, j] = len(position)
    return position


def camera_solve(load):
    position = pair_positions()
    factor, inverse = {}, []
    for j in range(CP):
        for i in range(j, CP):
            amount = load(position[j, i])
            if i == j:
                amount = amount + LM_LAMBDA
            for k in range(j):
                amount = amount - factor[k, j] * factor[k, i]
            if i == j:
                factor[j, j] = jnp.sqrt(amount)
                inverse.append(1.0 / factor[j, j])
            else:
                factor[j, i] = amount * inverse[j]
    forward = []
    for j in range(CP):
        amount = load(PACKED + j)
        for k in range(j):
            amount = amount - factor[k, j] * forward[k]
        forward.append(amount * inverse[j])
    backward = [None] * CP
    for i in range(CP - 1, -1, -1):
        amount = forward[i]
        for j in range(i + 1, CP):
            amount = amount - factor[i, j] * backward[j]
        backward[i] = amount * inverse[i]
    return [factor[i, j] for i in range(CP) for j in range(i, CP)], [-v for v in backward]


def fill_onehot(cam, onehot):
    for t in range(NOBS // 256):
        lane = cam[0:1, t * 256 : (t + 1) * 256] & 255
        hit = lax.broadcasted_iota(jnp.int32, (256, 256), 0) == lane
        onehot[:, t * 256 : (t + 1) * 256] = hit.astype(f32).astype(bf16)


PLANE = sorted(((a, b) for a in range(4) for b in range(4)), key=lambda q: -min(q[0], 4 - q[0]) - min(q[1], 4 - q[1]))
OWNERS = 14


def camera_kernel(
    rec, cam, fac_out, steps, pick,
    onehot, lhs, away, home, from_core, arrived, full, spread,
    send_a, recv_a, send_c, recv_c, send_d, recv_d, send_e, recv_e,
):
    img, mine = lax.axis_index("img"), lax.axis_index("cam")
    z, x, y, core = img // 4, img % 4, mine // 2, mine % 2

    def plane(q):
        return ((z + q[0]) % 4) * 4 + (x + q[1]) % 4

    barrier = pltpu.get_barrier_semaphore()
    pl.semaphore_signal(barrier, inc=1, device_id=(img, y * 2 + 1 - core), device_id_type=MESH)
    for dy in range(4):
        for q in PLANE:
            if dy or q != (0, 0):
                pl.semaphore_signal(
                    barrier, inc=1, device_id=(plane(q), ((y + dy) % 4) * 2 + core), device_id_type=MESH
                )
    for dy in range(1, 4):
        pl.semaphore_signal(
            barrier, inc=1, device_id=(img, ((y + dy) % 4) * 2 + 1 - core), device_id_type=MESH
        )

    fill_onehot(cam, onehot)

    def sums_of(owner):
        for half in range(2):
            for t in range(6):
                cols = slice(t * 512, (t + 1) * 512)
                hit = (cam[0:1, cols] >> 8) == owner * 2 + half
                mask = jnp.broadcast_to(hit.astype(f32), (16, 512)).astype(bf16)
                mask = jnp.concatenate([mask] * 7, axis=0)
                lhs[half * 112 : (half + 1) * 112, cols] = rec[:, cols] * mask
        r = lax.dot_general(
            lhs[...], onehot[...], (((1,), (1,)), ((), ())), preferred_element_type=f32
        )
        return [r[112 * h : 112 * h + 56] + r[112 * h + 56 : 112 * h + 112] for h in range(2)]

    ORDER = (2, 1, 3, 0)

    def core_copy(d):
        return pltpu.make_async_remote_copy(
            src_ref=away.at[d, pl.ds(0, OWNERS)], dst_ref=from_core.at[d, pl.ds(0, OWNERS)],
            send_sem=send_a.at[d], recv_sem=recv_a.at[d],
            device_id=(img, y * 2 + 1 - core), device_id_type=MESH,
        )

    def other_core(d):
        sums = sums_of(((y + ORDER[d]) % 4) * 2 + 1 - core)
        for h in range(2):
            for r in range(7):
                away[d, h * 7 + r] = sums[h][8 * r : 8 * r + 8]
        if d == 0:
            pl.semaphore_wait(barrier, 67)
        core_copy(d).start()

    def slice_copy(d, q):
        n = ORDER[d] * 16 + q[0] * 4 + q[1]
        return pltpu.make_async_remote_copy(
            src_ref=home.at[d, plane(q)], dst_ref=arrived.at[n],
            send_sem=send_c.at[n], recv_sem=recv_c.at[n],
            device_id=(plane(q), ((y + ORDER[d]) % 4) * 2 + core), device_id_type=MESH,
        )

    def own_core(d):
        sums = sums_of(((y + ORDER[d]) % 4) * 2 + core)
        core_copy(d).wait_recv()
        for h in range(2):
            for r in range(7):
                home[d, h * 7 + r] = sums[h][8 * r : 8 * r + 8] + from_core[d, h * 7 + r]
        for q in PLANE:
            if ORDER[d] or q != (0, 0):
                @pl.when(plane(q) < OWNERS)
                def _(q=q):
                    slice_copy(d, q).start()

    other_core(0)
    other_core(1)
    own_core(0)
    other_core(2)
    own_core(1)
    other_core(3)
    own_core(2)
    own_core(3)

    def sum_copy(q):
        n = q[0] * 4 + q[1]
        return pltpu.make_async_remote_copy(
            src_ref=full.at[img], dst_ref=full.at[img],
            send_sem=send_d.at[n], recv_sem=recv_d.at[n],
            device_id=(plane(q), mine), device_id_type=MESH,
        )

    @pl.when(img < OWNERS)
    def _():
        total = home[3, img]
        for d in range(4):
            for q in PLANE:
                if ORDER[d] or q != (0, 0):
                    slice_copy(d, q).wait_recv()
                    total = total + arrived[ORDER[d] * 16 + q[0] * 4 + q[1]]
        full[img] = total
        for q in PLANE[:15]:
            sum_copy(q).start()

    for t in range(NOBS // 256):
        cols = slice(t * 256, (t + 1) * 256)
        hit = lax.broadcasted_iota(jnp.int32, (128, 256), 0) == (cam[0:1, cols] & 127)
        hit = hit.astype(f32).astype(bf16)
        pick[0:128, cols] = hit
        pick[128:256, cols] = hit

    for q in PLANE[:15]:
        @pl.when(plane(((4 - q[0]) % 4, (4 - q[1]) % 4)) < OWNERS)
        def _(q=q):
            sum_copy(q).wait_recv()

    for h in range(2):
        for r in range(7):
            for e in range(2):
                spread[pl.ds(r * 32 + h * 2 + e, 8, stride=4), :] = full[h * 7 + r, :, e * 128 : (e + 1) * 128]
    factor, step = camera_solve(lambda c: spread[4 * c : 4 * c + 4, :])
    for n, v in enumerate(step):
        steps[mine, 4 * n : 4 * n + 4, :] = v
    steps[mine, 36:40, :] = jnp.zeros((4, 128), f32)

    to_cams = []
    for d in (4, 5, 3, 2, 6, 7, 1):
        copy = pltpu.make_async_remote_copy(
            src_ref=steps.at[mine], dst_ref=steps.at[mine],
            send_sem=send_e.at[d], recv_sem=recv_e.at[d],
            device_id=(img, (mine + d) % 8), device_id_type=MESH,
        )
        copy.start()
        to_cams.append(copy)

    for n, v in enumerate(factor):
        for q in range(4):
            fac_out[n : n + 1, q * 128 : (q + 1) * 128] = v[q : q + 1]

    for d in range(4):
        core_copy(d).wait_send()
        for q in PLANE:
            if ORDER[d] or q != (0, 0):
                @pl.when(plane(q) < OWNERS)
                def _(d=d, q=q):
                    slice_copy(d, q).wait_send()

    @pl.when(img < OWNERS)
    def _():
        for q in PLANE[:15]:
            sum_copy(q).wait_send()

    for copy in to_cams:
        copy.wait_recv()
    for copy in to_cams:
        copy.wait_send()


def camera_update(records, cam):
    vmem = pl.BlockSpec(memory_space=pltpu.MemorySpace.VMEM)
    dma = pltpu.SemaphoreType.DMA
    return pl.pallas_call(
        camera_kernel,
        out_shape=(
            jax.ShapeDtypeStruct((PACKED, 512), f32),
            jax.ShapeDtypeStruct((8, 40, 128), f32),
            jax.ShapeDtypeStruct((256, NOBS), bf16),
        ),
        in_specs=[vmem, vmem],
        out_specs=(vmem,) * 3,
        scratch_shapes=[
            pltpu.VMEM((256, NOBS), bf16),
            pltpu.VMEM((224, NOBS), bf16),
            pltpu.VMEM((4, 16, 8, 256), f32),
            pltpu.VMEM((4, 16, 8, 256), f32),
            pltpu.VMEM((4, 16, 8, 256), f32),
            pltpu.VMEM((64, 8, 256), f32),
            pltpu.VMEM((NIMG, 8, 256), f32),
            pltpu.VMEM((ROWS * 4, 128), f32),
            dma((4,)), dma((4,)), dma((64,)), dma((64,)), dma((NIMG,)), dma((NIMG,)), dma((8,)), dma((8,)),
        ],
        compiler_params=pltpu.CompilerParams(
            collective_id=0, has_side_effects=True, vmem_limit_bytes=40 << 20
        ),
        name="camera_update",
    )(records, cam)


def point_kernel(fac, steps, pick, cam, coup, small, fac_out, step_out, point_out, picked, groups):
    mine = lax.axis_index("cam")
    fac_out[...] = fac[...]
    for c in range(CP):
        for q in range(4):
            step_out[c : c + 1, q * 128 : (q + 1) * 128] = steps[mine, 4 * c + q : 4 * c + q + 1, :]
    table = steps[...].reshape(320, 128)
    high = table.astype(bf16).astype(f32)
    table = jnp.concatenate([high, table - high], axis=1).astype(bf16)
    quarter = lax.broadcasted_iota(jnp.int32, (40, 256), 0) & 3
    for b in range(NB):
        for q in range(4):
            cols = slice(b * 1024 + q * 256, b * 1024 + (q + 1) * 256)
            chosen = jnp.dot(table, pick[:, cols], preferred_element_type=f32)
            place = (cam[0:1, cols] >> 7) - quarter
            total = jnp.zeros((40, 256), f32)
            for g in range(8):
                total = total + jnp.where(place == 4 * g, chosen[40 * g : 40 * g + 40], 0.0)
            for e in range(2):
                groups[q * 2 + e] = total[:, e * 128 : (e + 1) * 128]
        for k in range(K):
            total = groups[k, pl.ds(0, 10, stride=4), :]
            for q in range(1, 4):
                total = total + groups[k, pl.ds(q, 10, stride=4), :]
            picked[pl.ds(k, 10, stride=8), :] = total
        sums = []
        for p in range(3):
            v = coup[b, p * CP] * picked[0:8, :]
            for c in range(1, CP):
                v = v + coup[b, p * CP + c] * picked[c * 8 : c * 8 + 8, :]
            sums.append(small[b, 6 + p : 7 + p, :] + jnp.sum(v, axis=0, keepdims=True))
        inv = [small[b, p : p + 1, :] for p in range(3)]
        r01, r02, r12 = [small[b, p : p + 1, :] for p in range(3, 6)]
        two = sums[2] * inv[2]
        one = (sums[1] - r12 * two) * inv[1]
        zero = (sums[0] - r01 * one - r02 * two) * inv[0]
        for p, v in enumerate((zero, one, two)):
            point_out[p : p + 1, b * 128 : (b + 1) * 128] = -v


def point_update(fac, steps, pick, cam, coup, small):
    vmem = pl.BlockSpec(memory_space=pltpu.MemorySpace.VMEM)
    return pl.pallas_call(
        point_kernel,
        out_shape=(
            jax.ShapeDtypeStruct((PACKED, 512), f32),
            jax.ShapeDtypeStruct((CP, 512), f32),
            jax.ShapeDtypeStruct((3, NL), f32),
        ),
        in_specs=[vmem] * 6,
        out_specs=(vmem,) * 3,
        scratch_shapes=[pltpu.VMEM((80, 128), f32), pltpu.VMEM((K, 40, 128), f32)],
        compiler_params=pltpu.CompilerParams(vmem_limit_bytes=32 << 20),
        name="point_update",
    )(fac, steps, pick, cam, coup, small)


def local(jac_cam, jac_point, residual, obs_count, obs_camera):
    records, coup, small, cam = marginalize(
        jnp.transpose(jac_cam, (0, 2, 1, 3)),
        jnp.transpose(jac_point, (0, 2, 1, 3)),
        residual,
        obs_count.reshape(NB, 128),
        jnp.transpose(obs_camera),
    )
    fac, steps, pick = camera_update(records, cam)
    return point_update(fac, steps, pick, cam, coup, small)


def solution(mesh):
    in_specs = (
        P(("img", "cam"), None, None, None),
        P(("img", "cam"), None, None, None),
        P(("img", "cam"), None, None),
        P(("img", "cam")),
        P(("img", "cam"), None),
    )
    out_specs = (P(None, "cam"), P(None, "cam"), P(None, ("img", "cam")))
    return jax.shard_map(local, mesh=mesh, in_specs=in_specs, out_specs=out_specs, check_vma=False)
```

```python
import functools

import jax
import jax.numpy as jnp
from jax import lax
from jax.experimental import pallas as pl
from jax.experimental.pallas import tpu as pltpu
from jax.sharding import PartitionSpec as P

CP = 9
K = 8
NL = 384
NB = 3
NOBS = NL * K
PACKED = 45
ROWS = 56
NIMG = 16
LM_LAMBDA = 0.5
f32 = jnp.float32
bf16 = jnp.bfloat16
MESH = pl.DeviceIdType.MESH

CC = [(i, j) for i in range(CP) for j in range(i, CP)]
CR = [(i, 9) for i in range(CP)]
QC = [(10 + p, c) for p in range(3) for c in range(CP)]
QR = [(10 + p, 9) for p in range(3)]
PAIRS = CC + CR + QC + QR
GROUPS = [PAIRS[0:28], PAIRS[28:56], PAIRS[56:84]]


def marginalize_kernel(
    jc, jp, rs, cnt_hbm, cam_hbm, ent_out, small_out, live_out, cam_out,
    jcv, jpv, rsv, qt, ta, tb, acc, cnt, cam, sem,
):
    def copy(b, which):
        s = pl.ds(b * 128, 128)
        src, dst = ((jp, jpv), (jc, jcv), (rs, rsv))[which]
        return pltpu.make_async_copy(src.at[s], dst.at[s], sem.at[b, which])

    count_copy = pltpu.make_async_copy(cnt_hbm, cnt, sem.at[NB, 0])
    cam_copy = pltpu.make_async_copy(cam_hbm, cam, sem.at[NB, 1])
    count_copy.start()
    for which in range(3):
        for b in range(NB):
            copy(b, which).start()
        if which == 0:
            cam_copy.start()
    count_copy.wait()

    jcf = jcv.reshape(NL * CP * K, 128)
    jpf = jpv.reshape(NL * 3 * K, 128)
    rsf = rsv.reshape(NL * K, 128)

    def point_phase(b, _):
        copy(b, 0).wait()
        count = cnt[pl.ds(b, 1), :]
        zero = jnp.zeros((8, 128), f32)

        def first(k, sums):
            live = (count > k).astype(f32)
            parts = []
            for p in range(3):
                v = jpf[pl.ds(b * (128 * 3 * K) + p * K + k, 128, stride=3 * K), :].T * live
                qt[p, b * K + k] = v
                parts.append(v)
            sums = list(sums)
            for x in range(16):
                a = [v[8 * x : 8 * x + 8] for v in parts]
                for q in range(3):
                    sums[q] = sums[q] + a[0] * a[q]
            return tuple(sums)

        s00, s01, s02 = [
            jnp.sum(v, axis=0, keepdims=True) for v in lax.fori_loop(0, K, first, (zero,) * 3)
        ]
        norm0 = jnp.sqrt(s00)
        inv0 = 1.0 / norm0
        r01 = s01 * inv0
        r02 = s02 * inv0
        c01 = r01 * inv0
        c02 = r02 * inv0

        def second(k, sums):
            n1, s12 = sums
            for x in range(16):
                rows = pl.ds(8 * x, 8)
                rem = qt[1, b * K + k, rows, :] - c01 * qt[0, b * K + k, rows, :]
                qt[1, b * K + k, rows, :] = rem
                n1 = n1 + rem * rem
                s12 = s12 + rem * qt[2, b * K + k, rows, :]
            return n1, s12

        n11, s12 = [
            jnp.sum(v, axis=0, keepdims=True) for v in lax.fori_loop(0, K, second, (zero,) * 2)
        ]
        norm1 = jnp.sqrt(n11)
        inv1 = 1.0 / norm1
        r12 = s12 * inv1
        c12 = r12 * inv1

        def third(k, n2):
            for x in range(16):
                rows = pl.ds(8 * x, 8)
                rem = (
                    qt[2, b * K + k, rows, :]
                    - c02 * qt[0, b * K + k, rows, :]
                    - c12 * qt[1, b * K + k, rows, :]
                )
                qt[2, b * K + k, rows, :] = rem
                n2 = n2 + rem * rem
            return n2

        n22 = jnp.sum(lax.fori_loop(0, K, third, zero), axis=0, keepdims=True)
        norm2 = jnp.sqrt(n22)
        inv2 = 1.0 / norm2
        for n, v in enumerate((inv0, inv1, inv2, r01, r02, r12)):
            small_out[b, n : n + 1, :] = v
        return 0

    lax.fori_loop(0, NB, point_phase, 0)

    def turn(b, k, t):
        for c in range(CP):
            t[c] = jcf[pl.ds(b * (128 * CP * K) + c * K + k, 128, stride=CP * K), :].T
        t[9] = rsf[pl.ds(b * (128 * K) + k, 128, stride=K), :].T

    def products(b, k, t):
        base = 0
        for pairs in GROUPS:
            total = [None] * len(pairs)
            for x in range(16):
                rows = pl.ds(8 * x, 8)
                held = {}
                for n, pair in enumerate(pairs):
                    for q in pair:
                        if q not in held:
                            held[q] = t[q, rows, :] if q < 10 else qt[q - 10, b * K + k, rows, :]
                    term = held[pair[0]] * held[pair[1]]
                    total[n] = term if total[n] is None else total[n] + term
            for n in range(len(pairs)):
                acc[base + n, pl.ds(pl.multiple_of(k * 8, 8), 8), :] = total[n]
            base += len(pairs)

    def camera_phase(b, _):
        copy(b, 1).wait()
        copy(b, 2).wait()
        turn(b, 0, ta)

        def two(h, _):
            turn(b, 2 * h + 1, tb)
            products(b, 2 * h, ta)
            turn(b, jnp.minimum(2 * h + 2, K - 1), ta)
            products(b, 2 * h + 1, tb)
            return 0

        lax.fori_loop(0, K // 2, two, 0)

        slot = lax.broadcasted_iota(jnp.int32, (8, 128), 0)
        live_out[b] = (slot < cnt[pl.ds(b, 1), :]).astype(f32)
        for n in range(len(PAIRS)):
            v = acc[n, pl.ds(0, 8, stride=8), :]
            for s in range(1, 8):
                v = v + acc[n, pl.ds(s, 8, stride=8), :]
            ent_out[b, n] = v
        return 0

    lax.fori_loop(0, NB, camera_phase, 0)
    cam_copy.wait()
    for b in range(NB):
        for k in range(K):
            cam_out[0:1, (b * K + k) * 128 : (b * K + k + 1) * 128] = cam[k : k + 1, b * 128 : (b + 1) * 128]


def marginalize(jac_cam, jac_point, residual, count, cam):
    hbm = pl.BlockSpec(memory_space=pltpu.MemorySpace.HBM)
    vmem = pl.BlockSpec(memory_space=pltpu.MemorySpace.VMEM)
    return pl.pallas_call(
        marginalize_kernel,
        out_shape=(
            jax.ShapeDtypeStruct((NB, len(PAIRS), 8, 128), f32),
            jax.ShapeDtypeStruct((NB, 16, 128), f32),
            jax.ShapeDtypeStruct((NB, 8, 128), f32),
            jax.ShapeDtypeStruct((1, NOBS), jnp.int32),
        ),
        in_specs=[hbm] * 5,
        out_specs=(vmem,) * 4,
        scratch_shapes=[
            pltpu.VMEM((NL, CP, K, 128), f32),
            pltpu.VMEM((NL, 3, K, 128), f32),
            pltpu.VMEM((NL, K, 128), f32),
            pltpu.VMEM((3, NB * K, 128, 128), f32),
            pltpu.VMEM((10, 128, 128), f32),
            pltpu.VMEM((10, 128, 128), f32),
            pltpu.VMEM((len(PAIRS), 64, 128), f32),
            pltpu.VMEM((NB, 128), jnp.int32),
            pltpu.VMEM((K, NL), jnp.int32),
            pltpu.SemaphoreType.DMA((NB + 1, 3)),
        ],
        compiler_params=pltpu.CompilerParams(vmem_limit_bytes=52 << 20),
        cost_estimate=pl.CostEstimate(flops=70_000_000, bytes_accessed=21_000_000, transcendentals=0),
        name="marginalize",
    )(jac_cam, jac_point, residual, count, cam)


def pair_positions():
    position = {}
    for i in range(CP):
        for j in range(i, CP):
            position[i, j] = len(position)
    return position


def camera_solve(load):
    position = pair_positions()
    factor, inverse = {}, []
    for j in range(CP):
        for i in range(j, CP):
            amount = load(position[j, i])
            if i == j:
                amount = amount + LM_LAMBDA
            for k in range(j):
                amount = amount - factor[k, j] * factor[k, i]
            if i == j:
                factor[j, j] = jnp.sqrt(amount)
                inverse.append(1.0 / factor[j, j])
            else:
                factor[j, i] = amount * inverse[j]
    forward = []
    for j in range(CP):
        amount = load(PACKED + j)
        for k in range(j):
            amount = amount - factor[k, j] * forward[k]
        forward.append(amount * inverse[j])
    backward = [None] * CP
    for i in range(CP - 1, -1, -1):
        amount = forward[i]
        for j in range(i + 1, CP):
            amount = amount - factor[i, j] * backward[j]
        backward[i] = amount * inverse[i]
    return [factor[i, j] for i in range(CP) for j in range(i, CP)], [-v for v in backward]


def fill_onehot(cam, onehot):
    for t in range(NOBS // 256):
        lane = cam[0:1, t * 256 : (t + 1) * 256] & 255
        hit = lax.broadcasted_iota(jnp.int32, (256, 256), 0) == lane
        onehot[:, t * 256 : (t + 1) * 256] = hit.astype(f32).astype(bf16)


PLANE = sorted(((a, b) for a in range(4) for b in range(4)), key=lambda q: -min(q[0], 4 - q[0]) - min(q[1], 4 - q[1]))
OWNERS = 14


def camera_kernel(
    ent, small, alive, cam, fac_out, steps, pick, coup_out, rhs_out,
    rec, turned, onehot, lhs, away, home, from_core, arrived, full, spread,
    send_a, recv_a, send_c, recv_c, send_d, recv_d, send_e, recv_e,
):
    img, mine = lax.axis_index("img"), lax.axis_index("cam")
    z, x, y, core = img // 4, img % 4, mine // 2, mine % 2

    def plane(q):
        return ((z + q[0]) % 4) * 4 + (x + q[1]) % 4

    barrier = pltpu.get_barrier_semaphore()
    pl.semaphore_signal(barrier, inc=1, device_id=(img, y * 2 + 1 - core), device_id_type=MESH)
    for dy in range(4):
        for q in PLANE:
            if dy or q != (0, 0):
                pl.semaphore_signal(
                    barrier, inc=1, device_id=(plane(q), ((y + dy) % 4) * 2 + core), device_id_type=MESH
                )
    for dy in range(1, 4):
        pl.semaphore_signal(
            barrier, inc=1, device_id=(img, ((y + dy) % 4) * 2 + 1 - core), device_id_type=MESH
        )

    def entry(b, n):
        return ent[b, n]

    def records(b, _):
        live = alive[b]
        inv = [small[b, p : p + 1, :] for p in range(3)]
        coupling = [[entry(b, 54 + p * CP + c) * inv[p] for c in range(CP)] for p in range(3)]
        for p in range(3):
            for c in range(CP):
                coup_out[b, p * CP + c] = coupling[p][c]
        rhs = [jnp.sum(entry(b, 81 + p), axis=0, keepdims=True) * inv[p] for p in range(3)]
        for p in range(3):
            rhs_out[b, p : p + 1, :] = rhs[p]
        for n, (i, j) in enumerate(CC):
            v = entry(b, n) * live
            for p in range(3):
                v = v - coupling[p][i] * coupling[p][j]
            turned[n * 8 : n * 8 + 8, :] = v
        for i in range(CP):
            v = entry(b, 45 + i) * live
            for p in range(3):
                v = v - coupling[p][i] * rhs[p]
            turned[(45 + i) * 8 : (45 + i) * 8 + 8, :] = v
        for i in range(54, ROWS):
            turned[i * 8 : i * 8 + 8, :] = jnp.zeros((8, 128), f32)
        for k in range(K):
            v = turned[pl.ds(k, ROWS, stride=8), :]
            high = v.astype(bf16).astype(f32)
            both = jnp.concatenate([high, v - high], axis=0).astype(bf16)
            rec[:, pl.ds(pl.multiple_of((b * K + k) * 128, 128), 128)] = both
        return 0

    lax.fori_loop(0, NB, records, 0)
    fill_onehot(cam, onehot)

    def sums_of(owner):
        for half in range(2):
            for t in range(6):
                cols = slice(t * 512, (t + 1) * 512)
                hit = (cam[0:1, cols] >> 8) == owner * 2 + half
                mask = jnp.broadcast_to(hit.astype(f32), (16, 512)).astype(bf16)
                mask = jnp.concatenate([mask] * 7, axis=0)
                lhs[half * 112 : (half + 1) * 112, cols] = rec[:, cols] * mask
        r = lax.dot_general(
            lhs[...], onehot[...], (((1,), (1,)), ((), ())), preferred_element_type=f32
        )
        return [r[112 * h : 112 * h + 56] + r[112 * h + 56 : 112 * h + 112] for h in range(2)]

    ORDER = (2, 1, 3, 0)

    def core_copy(d):
        return pltpu.make_async_remote_copy(
            src_ref=away.at[d, pl.ds(0, OWNERS)], dst_ref=from_core.at[d, pl.ds(0, OWNERS)],
            send_sem=send_a.at[d], recv_sem=recv_a.at[d],
            device_id=(img, y * 2 + 1 - core), device_id_type=MESH,
        )

    def other_core(d):
        sums = sums_of(((y + ORDER[d]) % 4) * 2 + 1 - core)
        for h in range(2):
            for r in range(7):
                away[d, h * 7 + r] = sums[h][8 * r : 8 * r + 8]

    def slice_copy(d, q):
        n = ORDER[d] * 16 + q[0] * 4 + q[1]
        return pltpu.make_async_remote_copy(
            src_ref=home.at[d, plane(q)], dst_ref=arrived.at[n],
            send_sem=send_c.at[n], recv_sem=recv_c.at[n],
            device_id=(plane(q), ((y + ORDER[d]) % 4) * 2 + core), device_id_type=MESH,
        )

    def own_core(d):
        sums = sums_of(((y + ORDER[d]) % 4) * 2 + core)
        core_copy(d).wait_recv()
        for h in range(2):
            for r in range(7):
                home[d, h * 7 + r] = sums[h][8 * r : 8 * r + 8] + from_core[d, h * 7 + r]
        for q in PLANE:
            if ORDER[d] or q != (0, 0):
                @pl.when(plane(q) < OWNERS)
                def _(q=q):
                    slice_copy(d, q).start()

    for d in range(4):
        other_core(d)
    pl.semaphore_wait(barrier, 67)
    for d in range(4):
        core_copy(d).start()
    for d in range(4):
        own_core(d)

    def sum_copy(q):
        n = q[0] * 4 + q[1]
        return pltpu.make_async_remote_copy(
            src_ref=full.at[img], dst_ref=full.at[img],
            send_sem=send_d.at[n], recv_sem=recv_d.at[n],
            device_id=(plane(q), mine), device_id_type=MESH,
        )

    @pl.when(img < OWNERS)
    def _():
        total = home[3, img]
        for d in range(4):
            for q in PLANE:
                if ORDER[d] or q != (0, 0):
                    slice_copy(d, q).wait_recv()
                    total = total + arrived[ORDER[d] * 16 + q[0] * 4 + q[1]]
        full[img] = total
        for q in PLANE[:15]:
            sum_copy(q).start()

    for t in range(NOBS // 256):
        cols = slice(t * 256, (t + 1) * 256)
        hit = lax.broadcasted_iota(jnp.int32, (128, 256), 0) == (cam[0:1, cols] & 127)
        hit = hit.astype(f32).astype(bf16)
        pick[0:128, cols] = hit
        pick[128:256, cols] = hit

    for q in PLANE[:15]:
        @pl.when(plane(((4 - q[0]) % 4, (4 - q[1]) % 4)) < OWNERS)
        def _(q=q):
            sum_copy(q).wait_recv()

    for h in range(2):
        for r in range(7):
            for e in range(2):
                spread[pl.ds(r * 32 + h * 2 + e, 8, stride=4), :] = full[h * 7 + r, :, e * 128 : (e + 1) * 128]
    factor, step = camera_solve(lambda c: spread[4 * c : 4 * c + 4, :])
    for n, v in enumerate(step):
        steps[mine, 4 * n : 4 * n + 4, :] = v
    steps[mine, 36:40, :] = jnp.zeros((4, 128), f32)

    to_cams = []
    for d in (4, 5, 3, 2, 6, 7, 1):
        copy = pltpu.make_async_remote_copy(
            src_ref=steps.at[mine], dst_ref=steps.at[mine],
            send_sem=send_e.at[d], recv_sem=recv_e.at[d],
            device_id=(img, (mine + d) % 8), device_id_type=MESH,
        )
        copy.start()
        to_cams.append(copy)

    for n, v in enumerate(factor):
        for q in range(4):
            fac_out[n : n + 1, q * 128 : (q + 1) * 128] = v[q : q + 1]

    for d in range(4):
        core_copy(d).wait_send()
        for q in PLANE:
            if ORDER[d] or q != (0, 0):
                @pl.when(plane(q) < OWNERS)
                def _(d=d, q=q):
                    slice_copy(d, q).wait_send()

    @pl.when(img < OWNERS)
    def _():
        for q in PLANE[:15]:
            sum_copy(q).wait_send()

    for copy in to_cams:
        copy.wait_recv()
    for copy in to_cams:
        copy.wait_send()


def camera_update(ent, small, alive, cam):
    vmem = pl.BlockSpec(memory_space=pltpu.MemorySpace.VMEM)
    dma = pltpu.SemaphoreType.DMA
    return pl.pallas_call(
        camera_kernel,
        out_shape=(
            jax.ShapeDtypeStruct((PACKED, 512), f32),
            jax.ShapeDtypeStruct((8, 40, 128), f32),
            jax.ShapeDtypeStruct((256, NOBS), bf16),
            jax.ShapeDtypeStruct((NB, 27, 8, 128), f32),
            jax.ShapeDtypeStruct((NB, 8, 128), f32),
        ),
        in_specs=[vmem] * 4,
        out_specs=(vmem,) * 5,
        scratch_shapes=[
            pltpu.VMEM((2 * ROWS, NOBS), bf16),
            pltpu.VMEM((ROWS * 8, 128), f32),
            pltpu.VMEM((256, NOBS), bf16),
            pltpu.VMEM((224, NOBS), bf16),
            pltpu.VMEM((4, 16, 8, 256), f32),
            pltpu.VMEM((4, 16, 8, 256), f32),
            pltpu.VMEM((4, 16, 8, 256), f32),
            pltpu.VMEM((64, 8, 256), f32),
            pltpu.VMEM((NIMG, 8, 256), f32),
            pltpu.VMEM((ROWS * 4, 128), f32),
            dma((4,)), dma((4,)), dma((64,)), dma((64,)), dma((NIMG,)), dma((NIMG,)), dma((8,)), dma((8,)),
        ],
        compiler_params=pltpu.CompilerParams(
            collective_id=0, has_side_effects=True, vmem_limit_bytes=40 << 20
        ),
        name="camera_update",
    )(ent, small, alive, cam)


def point_kernel(fac, steps, pick, cam, coup, small, rhs, fac_out, step_out, point_out, picked, groups):
    mine = lax.axis_index("cam")
    fac_out[...] = fac[...]
    for c in range(CP):
        for q in range(4):
            step_out[c : c + 1, q * 128 : (q + 1) * 128] = steps[mine, 4 * c + q : 4 * c + q + 1, :]
    table = steps[...].reshape(320, 128)
    high = table.astype(bf16).astype(f32)
    table = jnp.concatenate([high, table - high], axis=1).astype(bf16)
    quarter = lax.broadcasted_iota(jnp.int32, (40, 256), 0) & 3
    for b in range(NB):
        for q in range(4):
            cols = slice(b * 1024 + q * 256, b * 1024 + (q + 1) * 256)
            chosen = jnp.dot(table, pick[:, cols], preferred_element_type=f32)
            place = (cam[0:1, cols] >> 7) - quarter
            total = jnp.zeros((40, 256), f32)
            for g in range(8):
                total = total + jnp.where(place == 4 * g, chosen[40 * g : 40 * g + 40], 0.0)
            for e in range(2):
                groups[q * 2 + e] = total[:, e * 128 : (e + 1) * 128]
        for k in range(K):
            total = groups[k, pl.ds(0, 10, stride=4), :]
            for q in range(1, 4):
                total = total + groups[k, pl.ds(q, 10, stride=4), :]
            picked[pl.ds(k, 10, stride=8), :] = total
        sums = []
        for p in range(3):
            v = coup[b, p * CP] * picked[0:8, :]
            for c in range(1, CP):
                v = v + coup[b, p * CP + c] * picked[c * 8 : c * 8 + 8, :]
            sums.append(rhs[b, p : p + 1, :] + jnp.sum(v, axis=0, keepdims=True))
        inv = [small[b, p : p + 1, :] for p in range(3)]
        r01, r02, r12 = [small[b, p : p + 1, :] for p in range(3, 6)]
        two = sums[2] * inv[2]
        one = (sums[1] - r12 * two) * inv[1]
        zero = (sums[0] - r01 * one - r02 * two) * inv[0]
        for p, v in enumerate((zero, one, two)):
            point_out[p : p + 1, b * 128 : (b + 1) * 128] = -v


def point_update(fac, steps, pick, cam, coup, small, rhs):
    vmem = pl.BlockSpec(memory_space=pltpu.MemorySpace.VMEM)
    return pl.pallas_call(
        point_kernel,
        out_shape=(
            jax.ShapeDtypeStruct((PACKED, 512), f32),
            jax.ShapeDtypeStruct((CP, 512), f32),
            jax.ShapeDtypeStruct((3, NL), f32),
        ),
        in_specs=[vmem] * 7,
        out_specs=(vmem,) * 3,
        scratch_shapes=[pltpu.VMEM((80, 128), f32), pltpu.VMEM((K, 40, 128), f32)],
        compiler_params=pltpu.CompilerParams(vmem_limit_bytes=32 << 20),
        name="point_update",
    )(fac, steps, pick, cam, coup, small, rhs)


def local(jac_cam, jac_point, residual, obs_count, obs_camera):
    ent, small, alive, cam = marginalize(
        jnp.transpose(jac_cam, (0, 2, 1, 3)),
        jnp.transpose(jac_point, (0, 2, 1, 3)),
        residual,
        obs_count.reshape(NB, 128),
        jnp.transpose(obs_camera),
    )
    fac, steps, pick, coup, rhs = camera_update(ent, small, alive, cam)
    return point_update(fac, steps, pick, cam, coup, small, rhs)


def solution(mesh):
    in_specs = (
        P(("img", "cam"), None, None, None),
        P(("img", "cam"), None, None, None),
        P(("img", "cam"), None, None),
        P(("img", "cam")),
        P(("img", "cam"), None),
    )
    out_specs = (P(None, "cam"), P(None, "cam"), P(None, ("img", "cam")))
    return jax.shard_map(local, mesh=mesh, in_specs=in_specs, out_specs=out_specs, check_vma=False)
```

```python
import functools

import jax
import jax.numpy as jnp
from jax import lax
from jax.experimental import pallas as pl
from jax.experimental.pallas import tpu as pltpu
from jax.sharding import PartitionSpec as P

CP = 9
K = 8
NL = 384
NB = 3
NOBS = NL * K
PACKED = 45
ROWS = 56
NIMG = 16
LM_LAMBDA = 0.5
f32 = jnp.float32
bf16 = jnp.bfloat16
MESH = pl.DeviceIdType.MESH

CC = [(i, j) for i in range(CP) for j in range(i, CP)]
CR = [(i, 9) for i in range(CP)]
QC = [(10 + p, c) for p in range(3) for c in range(CP)]
QR = [(10 + p, 9) for p in range(3)]
PAIRS = CC + CR + QC + QR
GROUPS = [PAIRS[0:28], PAIRS[28:56], PAIRS[56:84]]


def pair_positions():
    position = {}
    for i in range(CP):
        for j in range(i, CP):
            position[i, j] = len(position)
    return position


def camera_solve(load):
    position = pair_positions()
    factor, inverse = {}, []
    for j in range(CP):
        for i in range(j, CP):
            amount = load(position[j, i])
            if i == j:
                amount = amount + LM_LAMBDA
            for k in range(j):
                amount = amount - factor[k, j] * factor[k, i]
            if i == j:
                factor[j, j] = jnp.sqrt(amount)
                inverse.append(1.0 / factor[j, j])
            else:
                factor[j, i] = amount * inverse[j]
    forward = []
    for j in range(CP):
        amount = load(PACKED + j)
        for k in range(j):
            amount = amount - factor[k, j] * forward[k]
        forward.append(amount * inverse[j])
    backward = [None] * CP
    for i in range(CP - 1, -1, -1):
        amount = forward[i]
        for j in range(i + 1, CP):
            amount = amount - factor[i, j] * backward[j]
        backward[i] = amount * inverse[i]
    return [factor[i, j] for i in range(CP) for j in range(i, CP)], [-v for v in backward]


def fill_onehot(cam, onehot):
    for t in range(NOBS // 256):
        lane = cam[0:1, t * 256 : (t + 1) * 256] & 255
        hit = lax.broadcasted_iota(jnp.int32, (256, 256), 0) == lane
        onehot[:, t * 256 : (t + 1) * 256] = hit.astype(f32).astype(bf16)


PLANE = sorted(((a, b) for a in range(4) for b in range(4)), key=lambda q: -min(q[0], 4 - q[0]) - min(q[1], 4 - q[1]))
OWNERS = 14


def camera_kernel(
    jc, jp, rs, cnt_hbm, cam_hbm, fac_out, steps, pick, coup_out, small_out, cam_out,
    jcv, jpv, rsv, qt, ta, tb, acc, cnt, cam, sem,
    rec, turned, onehot, lhs, away, home, from_core, arrived, full, spread,
    send_a, recv_a, send_c, recv_c, send_d, recv_d, send_e, recv_e,
):
    img, mine = lax.axis_index("img"), lax.axis_index("cam")
    z, x, y, core = img // 4, img % 4, mine // 2, mine % 2

    def plane(q):
        return ((z + q[0]) % 4) * 4 + (x + q[1]) % 4

    barrier = pltpu.get_barrier_semaphore()
    pl.semaphore_signal(barrier, inc=1, device_id=(img, y * 2 + 1 - core), device_id_type=MESH)
    for dy in range(4):
        for q in PLANE:
            if dy or q != (0, 0):
                pl.semaphore_signal(
                    barrier, inc=1, device_id=(plane(q), ((y + dy) % 4) * 2 + core), device_id_type=MESH
                )
    for dy in range(1, 4):
        pl.semaphore_signal(
            barrier, inc=1, device_id=(img, ((y + dy) % 4) * 2 + 1 - core), device_id_type=MESH
        )

    def copy(b, which):
        s = pl.ds(b * 128, 128)
        src, dst = ((jp, jpv), (jc, jcv), (rs, rsv))[which]
        return pltpu.make_async_copy(src.at[s], dst.at[s], sem.at[b, which])

    count_copy = pltpu.make_async_copy(cnt_hbm, cnt, sem.at[NB, 0])
    cam_copy = pltpu.make_async_copy(cam_hbm, cam, sem.at[NB, 1])
    count_copy.start()
    for which in range(3):
        for b in range(NB):
            copy(b, which).start()
        if which == 0:
            cam_copy.start()
    count_copy.wait()

    jcf = jcv.reshape(NL * CP * K, 128)
    jpf = jpv.reshape(NL * 3 * K, 128)
    rsf = rsv.reshape(NL * K, 128)

    def point_phase(b, _):
        copy(b, 0).wait()
        count = cnt[pl.ds(b, 1), :]
        zero = jnp.zeros((8, 128), f32)

        def first(k, sums):
            live = (count > k).astype(f32)
            parts = []
            for p in range(3):
                v = jpf[pl.ds(b * (128 * 3 * K) + p * K + k, 128, stride=3 * K), :].T * live
                qt[p, b * K + k] = v
                parts.append(v)
            sums = list(sums)
            for x in range(16):
                a = [v[8 * x : 8 * x + 8] for v in parts]
                for q in range(3):
                    sums[q] = sums[q] + a[0] * a[q]
            return tuple(sums)

        s00, s01, s02 = [
            jnp.sum(v, axis=0, keepdims=True) for v in lax.fori_loop(0, K, first, (zero,) * 3)
        ]
        norm0 = jnp.sqrt(s00)
        inv0 = 1.0 / norm0
        r01 = s01 * inv0
        r02 = s02 * inv0
        c01 = r01 * inv0
        c02 = r02 * inv0

        def second(k, sums):
            n1, s12 = sums
            for x in range(16):
                rows = pl.ds(8 * x, 8)
                rem = qt[1, b * K + k, rows, :] - c01 * qt[0, b * K + k, rows, :]
                qt[1, b * K + k, rows, :] = rem
                n1 = n1 + rem * rem
                s12 = s12 + rem * qt[2, b * K + k, rows, :]
            return n1, s12

        n11, s12 = [
            jnp.sum(v, axis=0, keepdims=True) for v in lax.fori_loop(0, K, second, (zero,) * 2)
        ]
        norm1 = jnp.sqrt(n11)
        inv1 = 1.0 / norm1
        r12 = s12 * inv1
        c12 = r12 * inv1

        def third(k, n2):
            for x in range(16):
                rows = pl.ds(8 * x, 8)
                rem = (
                    qt[2, b * K + k, rows, :]
                    - c02 * qt[0, b * K + k, rows, :]
                    - c12 * qt[1, b * K + k, rows, :]
                )
                qt[2, b * K + k, rows, :] = rem
                n2 = n2 + rem * rem
            return n2

        n22 = jnp.sum(lax.fori_loop(0, K, third, zero), axis=0, keepdims=True)
        norm2 = jnp.sqrt(n22)
        inv2 = 1.0 / norm2
        for n, v in enumerate((inv0, inv1, inv2, r01, r02, r12)):
            small_out[b, n : n + 1, :] = v
        return 0

    lax.fori_loop(0, NB, point_phase, 0)

    def turn(b, k, t):
        for c in range(CP):
            t[c] = jcf[pl.ds(b * (128 * CP * K) + c * K + k, 128, stride=CP * K), :].T
        t[9] = rsf[pl.ds(b * (128 * K) + k, 128, stride=K), :].T

    def products(b, k, t):
        base = 0
        for pairs in GROUPS:
            total = [None] * len(pairs)
            for x in range(16):
                rows = pl.ds(8 * x, 8)
                held = {}
                for n, pair in enumerate(pairs):
                    for q in pair:
                        if q not in held:
                            held[q] = t[q, rows, :] if q < 10 else qt[q - 10, b * K + k, rows, :]
                    term = held[pair[0]] * held[pair[1]]
                    total[n] = term if total[n] is None else total[n] + term
            for n in range(len(pairs)):
                acc[base + n, pl.ds(pl.multiple_of(k * 8, 8), 8), :] = total[n]
            base += len(pairs)

    def camera_phase(b, _):
        copy(b, 1).wait()
        copy(b, 2).wait()
        turn(b, 0, ta)

        def two(h, _):
            turn(b, 2 * h + 1, tb)
            products(b, 2 * h, ta)
            turn(b, jnp.minimum(2 * h + 2, K - 1), ta)
            products(b, 2 * h + 1, tb)
            return 0

        lax.fori_loop(0, K // 2, two, 0)

        def entry(n):
            v = acc[n, pl.ds(0, 8, stride=8), :]
            for s in range(1, 8):
                v = v + acc[n, pl.ds(s, 8, stride=8), :]
            return v

        slot = lax.broadcasted_iota(jnp.int32, (8, 128), 0)
        live = (slot < cnt[pl.ds(b, 1), :]).astype(f32)
        inv = [small_out[b, p : p + 1, :] for p in range(3)]
        coupling = [[entry(54 + p * CP + c) * inv[p] for c in range(CP)] for p in range(3)]
        for p in range(3):
            for c in range(CP):
                coup_out[b, p * CP + c] = coupling[p][c]
        rhs = [jnp.sum(entry(81 + p), axis=0, keepdims=True) * inv[p] for p in range(3)]
        for p in range(3):
            small_out[b, 6 + p : 7 + p, :] = rhs[p]
        for n, (i, j) in enumerate(CC):
            v = entry(n) * live
            for p in range(3):
                v = v - coupling[p][i] * coupling[p][j]
            turned[n * 8 : n * 8 + 8, :] = v
        for i in range(CP):
            v = entry(45 + i) * live
            for p in range(3):
                v = v - coupling[p][i] * rhs[p]
            turned[(45 + i) * 8 : (45 + i) * 8 + 8, :] = v
        for i in range(54, ROWS):
            turned[i * 8 : i * 8 + 8, :] = jnp.zeros((8, 128), f32)
        for k in range(K):
            v = turned[pl.ds(k, ROWS, stride=8), :]
            high = v.astype(bf16).astype(f32)
            both = jnp.concatenate([high, v - high], axis=0).astype(bf16)
            rec[:, pl.ds(pl.multiple_of((b * K + k) * 128, 128), 128)] = both
        return 0

    lax.fori_loop(0, NB, camera_phase, 0)
    cam_copy.wait()
    for b in range(NB):
        for k in range(K):
            cam_out[0:1, (b * K + k) * 128 : (b * K + k + 1) * 128] = cam[k : k + 1, b * 128 : (b + 1) * 128]

    fill_onehot(cam_out, onehot)

    def sums_of(owner):
        for half in range(2):
            for t in range(6):
                cols = slice(t * 512, (t + 1) * 512)
                hit = (cam_out[0:1, cols] >> 8) == owner * 2 + half
                mask = jnp.broadcast_to(hit.astype(f32), (16, 512)).astype(bf16)
                mask = jnp.concatenate([mask] * 7, axis=0)
                lhs[half * 112 : (half + 1) * 112, cols] = rec[:, cols] * mask
        r = lax.dot_general(
            lhs[...], onehot[...], (((1,), (1,)), ((), ())), preferred_element_type=f32
        )
        return [r[112 * h : 112 * h + 56] + r[112 * h + 56 : 112 * h + 112] for h in range(2)]

    ORDER = (2, 1, 3, 0)

    def core_copy(d):
        return pltpu.make_async_remote_copy(
            src_ref=away.at[d, pl.ds(0, OWNERS)], dst_ref=from_core.at[d, pl.ds(0, OWNERS)],
            send_sem=send_a.at[d], recv_sem=recv_a.at[d],
            device_id=(img, y * 2 + 1 - core), device_id_type=MESH,
        )

    def other_core(d):
        sums = sums_of(((y + ORDER[d]) % 4) * 2 + 1 - core)
        for h in range(2):
            for r in range(7):
                away[d, h * 7 + r] = sums[h][8 * r : 8 * r + 8]
        core_copy(d).start()

    def slice_copy(d, q):
        n = ORDER[d] * 16 + q[0] * 4 + q[1]
        return pltpu.make_async_remote_copy(
            src_ref=home.at[d, plane(q)], dst_ref=arrived.at[n],
            send_sem=send_c.at[n], recv_sem=recv_c.at[n],
            device_id=(plane(q), ((y + ORDER[d]) % 4) * 2 + core), device_id_type=MESH,
        )

    def own_core(d):
        sums = sums_of(((y + ORDER[d]) % 4) * 2 + core)
        core_copy(d).wait_recv()
        for h in range(2):
            for r in range(7):
                home[d, h * 7 + r] = sums[h][8 * r : 8 * r + 8] + from_core[d, h * 7 + r]
        for q in PLANE:
            if ORDER[d] or q != (0, 0):
                @pl.when(plane(q) < OWNERS)
                def _(q=q):
                    slice_copy(d, q).start()

    pl.semaphore_wait(barrier, 67)
    other_core(0)
    other_core(1)
    own_core(0)
    other_core(2)
    own_core(1)
    other_core(3)
    own_core(2)
    own_core(3)

    def sum_copy(q):
        n = q[0] * 4 + q[1]
        return pltpu.make_async_remote_copy(
            src_ref=full.at[img], dst_ref=full.at[img],
            send_sem=send_d.at[n], recv_sem=recv_d.at[n],
            device_id=(plane(q), mine), device_id_type=MESH,
        )

    @pl.when(img < OWNERS)
    def _():
        total = home[3, img]
        for d in range(4):
            for q in PLANE:
                if ORDER[d] or q != (0, 0):
                    slice_copy(d, q).wait_recv()
                    total = total + arrived[ORDER[d] * 16 + q[0] * 4 + q[1]]
        full[img] = total
        for q in PLANE[:15]:
            sum_copy(q).start()

    for t in range(NOBS // 256):
        cols = slice(t * 256, (t + 1) * 256)
        hit = lax.broadcasted_iota(jnp.int32, (128, 256), 0) == (cam_out[0:1, cols] & 127)
        hit = hit.astype(f32).astype(bf16)
        pick[0:128, cols] = hit
        pick[128:256, cols] = hit

    for q in PLANE[:15]:
        @pl.when(plane(((4 - q[0]) % 4, (4 - q[1]) % 4)) < OWNERS)
        def _(q=q):
            sum_copy(q).wait_recv()

    for h in range(2):
        for r in range(7):
            for e in range(2):
                spread[pl.ds(r * 32 + h * 2 + e, 8, stride=4), :] = full[h * 7 + r, :, e * 128 : (e + 1) * 128]
    factor, step = camera_solve(lambda c: spread[4 * c : 4 * c + 4, :])
    for n, v in enumerate(step):
        steps[mine, 4 * n : 4 * n + 4, :] = v
    steps[mine, 36:40, :] = jnp.zeros((4, 128), f32)

    to_cams = []
    for d in (4, 5, 3, 2, 6, 7, 1):
        copy = pltpu.make_async_remote_copy(
            src_ref=steps.at[mine], dst_ref=steps.at[mine],
            send_sem=send_e.at[d], recv_sem=recv_e.at[d],
            device_id=(img, (mine + d) % 8), device_id_type=MESH,
        )
        copy.start()
        to_cams.append(copy)

    for n, v in enumerate(factor):
        for q in range(4):
            fac_out[n : n + 1, q * 128 : (q + 1) * 128] = v[q : q + 1]

    for d in range(4):
        core_copy(d).wait_send()
        for q in PLANE:
            if ORDER[d] or q != (0, 0):
                @pl.when(plane(q) < OWNERS)
                def _(d=d, q=q):
                    slice_copy(d, q).wait_send()

    @pl.when(img < OWNERS)
    def _():
        for q in PLANE[:15]:
            sum_copy(q).wait_send()

    for copy in to_cams:
        copy.wait_recv()
    for copy in to_cams:
        copy.wait_send()


def camera_update(jac_cam, jac_point, residual, count, cam):
    hbm = pl.BlockSpec(memory_space=pltpu.MemorySpace.HBM)
    vmem = pl.BlockSpec(memory_space=pltpu.MemorySpace.VMEM)
    dma = pltpu.SemaphoreType.DMA
    return pl.pallas_call(
        camera_kernel,
        out_shape=(
            jax.ShapeDtypeStruct((PACKED, 512), f32),
            jax.ShapeDtypeStruct((8, 40, 128), f32),
            jax.ShapeDtypeStruct((256, NOBS), bf16),
            jax.ShapeDtypeStruct((NB, 27, 8, 128), f32),
            jax.ShapeDtypeStruct((NB, 16, 128), f32),
            jax.ShapeDtypeStruct((1, NOBS), jnp.int32),
        ),
        in_specs=[hbm] * 5,
        out_specs=(vmem,) * 6,
        scratch_shapes=[
            pltpu.VMEM((NL, CP, K, 128), f32),
            pltpu.VMEM((NL, 3, K, 128), f32),
            pltpu.VMEM((NL, K, 128), f32),
            pltpu.VMEM((3, NB * K, 128, 128), f32),
            pltpu.VMEM((10, 128, 128), f32),
            pltpu.VMEM((10, 128, 128), f32),
            pltpu.VMEM((len(PAIRS), 64, 128), f32),
            pltpu.VMEM((NB, 128), jnp.int32),
            pltpu.VMEM((K, NL), jnp.int32),
            pltpu.SemaphoreType.DMA((NB + 1, 3)),
            pltpu.VMEM((2 * ROWS, NOBS), bf16),
            pltpu.VMEM((ROWS * 8, 128), f32),
            pltpu.VMEM((256, NOBS), bf16),
            pltpu.VMEM((224, NOBS), bf16),
            pltpu.VMEM((4, 16, 8, 256), f32),
            pltpu.VMEM((4, 16, 8, 256), f32),
            pltpu.VMEM((4, 16, 8, 256), f32),
            pltpu.VMEM((64, 8, 256), f32),
            pltpu.VMEM((NIMG, 8, 256), f32),
            pltpu.VMEM((ROWS * 4, 128), f32),
            dma((4,)), dma((4,)), dma((64,)), dma((64,)), dma((NIMG,)), dma((NIMG,)), dma((8,)), dma((8,)),
        ],
        compiler_params=pltpu.CompilerParams(
            collective_id=0, has_side_effects=True, vmem_limit_bytes=50 << 20
        ),
        name="marginalize_and_sum",
    )(jac_cam, jac_point, residual, count, cam)


def point_kernel(fac, steps, pick, cam, coup, small, fac_out, step_out, point_out, picked, groups):
    mine = lax.axis_index("cam")
    fac_out[...] = fac[...]
    for c in range(CP):
        for q in range(4):
            step_out[c : c + 1, q * 128 : (q + 1) * 128] = steps[mine, 4 * c + q : 4 * c + q + 1, :]
    table = steps[...].reshape(320, 128)
    high = table.astype(bf16).astype(f32)
    table = jnp.concatenate([high, table - high], axis=1).astype(bf16)
    quarter = lax.broadcasted_iota(jnp.int32, (40, 256), 0) & 3
    for b in range(NB):
        for q in range(4):
            cols = slice(b * 1024 + q * 256, b * 1024 + (q + 1) * 256)
            chosen = jnp.dot(table, pick[:, cols], preferred_element_type=f32)
            place = (cam[0:1, cols] >> 7) - quarter
            total = jnp.zeros((40, 256), f32)
            for g in range(8):
                total = total + jnp.where(place == 4 * g, chosen[40 * g : 40 * g + 40], 0.0)
            for e in range(2):
                groups[q * 2 + e] = total[:, e * 128 : (e + 1) * 128]
        for k in range(K):
            total = groups[k, pl.ds(0, 10, stride=4), :]
            for q in range(1, 4):
                total = total + groups[k, pl.ds(q, 10, stride=4), :]
            picked[pl.ds(k, 10, stride=8), :] = total
        sums = []
        for p in range(3):
            v = coup[b, p * CP] * picked[0:8, :]
            for c in range(1, CP):
                v = v + coup[b, p * CP + c] * picked[c * 8 : c * 8 + 8, :]
            sums.append(small[b, 6 + p : 7 + p, :] + jnp.sum(v, axis=0, keepdims=True))
        inv = [small[b, p : p + 1, :] for p in range(3)]
        r01, r02, r12 = [small[b, p : p + 1, :] for p in range(3, 6)]
        two = sums[2] * inv[2]
        one = (sums[1] - r12 * two) * inv[1]
        zero = (sums[0] - r01 * one - r02 * two) * inv[0]
        for p, v in enumerate((zero, one, two)):
            point_out[p : p + 1, b * 128 : (b + 1) * 128] = -v


def point_update(fac, steps, pick, cam, coup, small):
    vmem = pl.BlockSpec(memory_space=pltpu.MemorySpace.VMEM)
    return pl.pallas_call(
        point_kernel,
        out_shape=(
            jax.ShapeDtypeStruct((PACKED, 512), f32),
            jax.ShapeDtypeStruct((CP, 512), f32),
            jax.ShapeDtypeStruct((3, NL), f32),
        ),
        in_specs=[vmem] * 6,
        out_specs=(vmem,) * 3,
        scratch_shapes=[pltpu.VMEM((80, 128), f32), pltpu.VMEM((K, 40, 128), f32)],
        compiler_params=pltpu.CompilerParams(vmem_limit_bytes=32 << 20),
        name="point_update",
    )(fac, steps, pick, cam, coup, small)


def local(jac_cam, jac_point, residual, obs_count, obs_camera):
    operands = (
        jnp.transpose(jac_cam, (0, 2, 1, 3)),
        jnp.transpose(jac_point, (0, 2, 1, 3)),
        residual,
        obs_count.reshape(NB, 128),
        jnp.transpose(obs_camera),
    )
    operands = [pltpu.with_memory_space_constraint(v, pltpu.MemorySpace.HBM) for v in operands]
    fac, steps, pick, coup, small, cam = camera_update(*operands)
    return point_update(fac, steps, pick, cam, coup, small)


def solution(mesh):
    in_specs = (
        P(("img", "cam"), None, None, None),
        P(("img", "cam"), None, None, None),
        P(("img", "cam"), None, None),
        P(("img", "cam")),
        P(("img", "cam"), None),
    )
    out_specs = (P(None, "cam"), P(None, "cam"), P(None, ("img", "cam")))
    return jax.shard_map(local, mesh=mesh, in_specs=in_specs, out_specs=out_specs, check_vma=False)
```

```python
import functools

import jax
import jax.numpy as jnp
from jax import lax
from jax.experimental import pallas as pl
from jax.experimental.pallas import tpu as pltpu
from jax.sharding import PartitionSpec as P

CP = 9
K = 8
NL = 384
NB = 3
NOBS = NL * K
PACKED = 45
ROWS = 56
NIMG = 16
LM_LAMBDA = 0.5
f32 = jnp.float32
bf16 = jnp.bfloat16
MESH = pl.DeviceIdType.MESH

CC = [(i, j) for i in range(CP) for j in range(i, CP)]
CR = [(i, 9) for i in range(CP)]
QC = [(10 + p, c) for p in range(3) for c in range(CP)]
QR = [(10 + p, 9) for p in range(3)]
PAIRS = CC + CR + QC + QR
GROUPS = [PAIRS[0:28], PAIRS[28:56], PAIRS[56:84]]


def pair_positions():
    position = {}
    for i in range(CP):
        for j in range(i, CP):
            position[i, j] = len(position)
    return position


def camera_solve(load):
    position = pair_positions()
    factor, inverse = {}, []
    for j in range(CP):
        for i in range(j, CP):
            amount = load(position[j, i])
            if i == j:
                amount = amount + LM_LAMBDA
            for k in range(j):
                amount = amount - factor[k, j] * factor[k, i]
            if i == j:
                factor[j, j] = jnp.sqrt(amount)
                inverse.append(1.0 / factor[j, j])
            else:
                factor[j, i] = amount * inverse[j]
    forward = []
    for j in range(CP):
        amount = load(PACKED + j)
        for k in range(j):
            amount = amount - factor[k, j] * forward[k]
        forward.append(amount * inverse[j])
    backward = [None] * CP
    for i in range(CP - 1, -1, -1):
        amount = forward[i]
        for j in range(i + 1, CP):
            amount = amount - factor[i, j] * backward[j]
        backward[i] = amount * inverse[i]
    return [factor[i, j] for i in range(CP) for j in range(i, CP)], [-v for v in backward]


def fill_onehot(cam, onehot):
    for t in range(NOBS // 256):
        lane = cam[0:1, t * 256 : (t + 1) * 256] & 255
        hit = lax.broadcasted_iota(jnp.int32, (256, 256), 0) == lane
        onehot[:, t * 256 : (t + 1) * 256] = hit.astype(f32).astype(bf16)


PLANE = sorted(((a, b) for a in range(4) for b in range(4)), key=lambda q: -min(q[0], 4 - q[0]) - min(q[1], 4 - q[1]))
OWNERS = 14


def camera_kernel(
    jc, jp, rs, cnt_hbm, cam_hbm, fac_out, steps, pick, coup_out, small_out, cam_out,
    jcv, jpv, rsv, qt, ta, tb, acc, cnt, cam, sem,
    rec, turned, onehot, lhs, away, home, from_core, arrived, full, spread,
    send_a, recv_a, send_c, recv_c, send_d, recv_d, send_e, recv_e,
):
    img, mine = lax.axis_index("img"), lax.axis_index("cam")
    z, x, y, core = img // 4, img % 4, mine // 2, mine % 2

    def plane(q):
        return ((z + q[0]) % 4) * 4 + (x + q[1]) % 4

    barrier = pltpu.get_barrier_semaphore()
    pl.semaphore_signal(barrier, inc=1, device_id=(img, y * 2 + 1 - core), device_id_type=MESH)
    for dy in range(4):
        for q in PLANE:
            if dy or q != (0, 0):
                pl.semaphore_signal(
                    barrier, inc=1, device_id=(plane(q), ((y + dy) % 4) * 2 + core), device_id_type=MESH
                )
    for dy in range(1, 4):
        pl.semaphore_signal(
            barrier, inc=1, device_id=(img, ((y + dy) % 4) * 2 + 1 - core), device_id_type=MESH
        )

    def copy(b, which):
        s = pl.ds(b * 128, 128)
        src, dst = ((jp, jpv), (jc, jcv), (rs, rsv))[which]
        return pltpu.make_async_copy(src.at[s], dst.at[s], sem.at[b, which])

    count_copy = pltpu.make_async_copy(cnt_hbm, cnt, sem.at[NB, 0])
    cam_copy = pltpu.make_async_copy(cam_hbm, cam, sem.at[NB, 1])
    count_copy.start()
    cam_copy.start()
    for which in range(3):
        for b in range(NB):
            copy(b, which).start()
    count_copy.wait()
    cam_copy.wait()
    for b in range(NB):
        for k in range(K):
            cam_out[0:1, (b * K + k) * 128 : (b * K + k + 1) * 128] = cam[k : k + 1, b * 128 : (b + 1) * 128]
    fill_onehot(cam_out, onehot)

    jcf = jcv.reshape(NL * CP * K, 128)
    jpf = jpv.reshape(NL * 3 * K, 128)
    rsf = rsv.reshape(NL * K, 128)

    def point_phase(b, _):
        copy(b, 0).wait()
        count = cnt[pl.ds(b, 1), :]
        zero = jnp.zeros((8, 128), f32)

        def first(k, sums):
            live = (count > k).astype(f32)
            parts = []
            for p in range(3):
                v = jpf[pl.ds(b * (128 * 3 * K) + p * K + k, 128, stride=3 * K), :].T * live
                qt[p, b * K + k] = v
                parts.append(v)
            sums = list(sums)
            for x in range(16):
                a = [v[8 * x : 8 * x + 8] for v in parts]
                for q in range(3):
                    sums[q] = sums[q] + a[0] * a[q]
            return tuple(sums)

        s00, s01, s02 = [
            jnp.sum(v, axis=0, keepdims=True) for v in lax.fori_loop(0, K, first, (zero,) * 3, unroll=K)
        ]
        norm0 = jnp.sqrt(s00)
        inv0 = 1.0 / norm0
        r01 = s01 * inv0
        r02 = s02 * inv0
        c01 = r01 * inv0
        c02 = r02 * inv0

        def second(k, sums):
            n1, s12 = sums
            for x in range(16):
                rows = pl.ds(8 * x, 8)
                rem = qt[1, b * K + k, rows, :] - c01 * qt[0, b * K + k, rows, :]
                qt[1, b * K + k, rows, :] = rem
                n1 = n1 + rem * rem
                s12 = s12 + rem * qt[2, b * K + k, rows, :]
            return n1, s12

        n11, s12 = [
            jnp.sum(v, axis=0, keepdims=True) for v in lax.fori_loop(0, K, second, (zero,) * 2, unroll=K)
        ]
        norm1 = jnp.sqrt(n11)
        inv1 = 1.0 / norm1
        r12 = s12 * inv1
        c12 = r12 * inv1

        def third(k, n2):
            for x in range(16):
                rows = pl.ds(8 * x, 8)
                rem = (
                    qt[2, b * K + k, rows, :]
                    - c02 * qt[0, b * K + k, rows, :]
                    - c12 * qt[1, b * K + k, rows, :]
                )
                qt[2, b * K + k, rows, :] = rem
                n2 = n2 + rem * rem
            return n2

        n22 = jnp.sum(lax.fori_loop(0, K, third, zero, unroll=K), axis=0, keepdims=True)
        norm2 = jnp.sqrt(n22)
        inv2 = 1.0 / norm2
        for n, v in enumerate((inv0, inv1, inv2, r01, r02, r12)):
            small_out[b, n : n + 1, :] = v
        return 0

    lax.fori_loop(0, NB, point_phase, 0)

    def turn(b, k, t):
        for c in range(CP):
            t[c] = jcf[pl.ds(b * (128 * CP * K) + c * K + k, 128, stride=CP * K), :].T
        t[9] = rsf[pl.ds(b * (128 * K) + k, 128, stride=K), :].T

    def products(b, k, t):
        base = 0
        for pairs in GROUPS:
            total = [None] * len(pairs)
            for x in range(16):
                rows = pl.ds(8 * x, 8)
                held = {}
                for n, pair in enumerate(pairs):
                    for q in pair:
                        if q not in held:
                            held[q] = t[q, rows, :] if q < 10 else qt[q - 10, b * K + k, rows, :]
                    term = held[pair[0]] * held[pair[1]]
                    total[n] = term if total[n] is None else total[n] + term
            for n in range(len(pairs)):
                acc[base + n, pl.ds(pl.multiple_of(k * 8, 8), 8), :] = total[n]
            base += len(pairs)

    def camera_phase(b, _):
        copy(b, 1).wait()
        copy(b, 2).wait()
        turn(b, 0, ta)

        def two(h, _):
            turn(b, 2 * h + 1, tb)
            products(b, 2 * h, ta)
            turn(b, jnp.minimum(2 * h + 2, K - 1), ta)
            products(b, 2 * h + 1, tb)
            return 0

        lax.fori_loop(0, K // 2, two, 0, unroll=2)

        def entry(n):
            v = acc[n, pl.ds(0, 8, stride=8), :]
            for s in range(1, 8):
                v = v + acc[n, pl.ds(s, 8, stride=8), :]
            return v

        slot = lax.broadcasted_iota(jnp.int32, (8, 128), 0)
        live = (slot < cnt[pl.ds(b, 1), :]).astype(f32)
        inv = [small_out[b, p : p + 1, :] for p in range(3)]
        coupling = [[entry(54 + p * CP + c) * inv[p] for c in range(CP)] for p in range(3)]
        for p in range(3):
            for c in range(CP):
                coup_out[b, p * CP + c] = coupling[p][c]
        rhs = [jnp.sum(entry(81 + p), axis=0, keepdims=True) * inv[p] for p in range(3)]
        for p in range(3):
            small_out[b, 6 + p : 7 + p, :] = rhs[p]
        for n, (i, j) in enumerate(CC):
            v = entry(n) * live
            for p in range(3):
                v = v - coupling[p][i] * coupling[p][j]
            turned[n * 8 : n * 8 + 8, :] = v
        for i in range(CP):
            v = entry(45 + i) * live
            for p in range(3):
                v = v - coupling[p][i] * rhs[p]
            turned[(45 + i) * 8 : (45 + i) * 8 + 8, :] = v
        for i in range(54, ROWS):
            turned[i * 8 : i * 8 + 8, :] = jnp.zeros((8, 128), f32)
        for k in range(K):
            v = turned[pl.ds(k, ROWS, stride=8), :]
            high = v.astype(bf16).astype(f32)
            both = jnp.concatenate([high, v - high], axis=0).astype(bf16)
            rec[:, pl.ds(pl.multiple_of((b * K + k) * 128, 128), 128)] = both
        return 0

    lax.fori_loop(0, NB, camera_phase, 0)

    def sums_of(owners):
        for n, owner in enumerate(owners):
            for half in range(2):
                rows = slice((n * 2 + half) * 112, (n * 2 + half + 1) * 112)
                for t in range(6):
                    cols = slice(t * 512, (t + 1) * 512)
                    hit = (cam_out[0:1, cols] >> 8) == owner * 2 + half
                    mask = jnp.broadcast_to(hit.astype(f32), (16, 512)).astype(bf16)
                    mask = jnp.concatenate([mask] * 7, axis=0)
                    lhs[rows, cols] = rec[:, cols] * mask
        r = lax.dot_general(
            lhs[...], onehot[...], (((1,), (1,)), ((), ())), preferred_element_type=f32
        )
        return [r[112 * h : 112 * h + 56] + r[112 * h + 56 : 112 * h + 112] for h in range(4)]

    ORDER = (2, 1, 3, 0)

    def core_copy(d):
        return pltpu.make_async_remote_copy(
            src_ref=away.at[d, pl.ds(0, OWNERS)], dst_ref=from_core.at[d, pl.ds(0, OWNERS)],
            send_sem=send_a.at[d], recv_sem=recv_a.at[d],
            device_id=(img, y * 2 + 1 - core), device_id_type=MESH,
        )

    def both_cores(d):
        to_y = (y + ORDER[d]) % 4
        sums = sums_of((to_y * 2 + 1 - core, to_y * 2 + core))
        for h in range(2):
            for r in range(7):
                away[d, h * 7 + r] = sums[h][8 * r : 8 * r + 8]
                home[d, h * 7 + r] = sums[2 + h][8 * r : 8 * r + 8]
        core_copy(d).start()

    def slice_copy(d, q):
        n = ORDER[d] * 16 + q[0] * 4 + q[1]
        return pltpu.make_async_remote_copy(
            src_ref=home.at[d, plane(q)], dst_ref=arrived.at[n],
            send_sem=send_c.at[n], recv_sem=recv_c.at[n],
            device_id=(plane(q), ((y + ORDER[d]) % 4) * 2 + core), device_id_type=MESH,
        )

    def send_on(d):
        core_copy(d).wait_recv()
        home[d, 0:OWNERS] = home[d, 0:OWNERS] + from_core[d, 0:OWNERS]
        for q in PLANE:
            if ORDER[d] or q != (0, 0):
                @pl.when(plane(q) < OWNERS)
                def _(q=q):
                    slice_copy(d, q).start()

    pl.semaphore_wait(barrier, 67)
    both_cores(0)
    for d in range(1, 4):
        both_cores(d)
        send_on(d - 1)
    send_on(3)

    def sum_copy(q):
        n = q[0] * 4 + q[1]
        return pltpu.make_async_remote_copy(
            src_ref=full.at[img], dst_ref=full.at[img],
            send_sem=send_d.at[n], recv_sem=recv_d.at[n],
            device_id=(plane(q), mine), device_id_type=MESH,
        )

    @pl.when(img < OWNERS)
    def _():
        total = home[3, img]
        for d in range(4):
            for q in PLANE:
                if ORDER[d] or q != (0, 0):
                    slice_copy(d, q).wait_recv()
                    total = total + arrived[ORDER[d] * 16 + q[0] * 4 + q[1]]
        full[img] = total
        for q in PLANE[:15]:
            sum_copy(q).start()

    for t in range(NOBS // 256):
        cols = slice(t * 256, (t + 1) * 256)
        hit = lax.broadcasted_iota(jnp.int32, (128, 256), 0) == (cam_out[0:1, cols] & 127)
        hit = hit.astype(f32).astype(bf16)
        pick[0:128, cols] = hit
        pick[128:256, cols] = hit

    for q in PLANE[:15]:
        @pl.when(plane(((4 - q[0]) % 4, (4 - q[1]) % 4)) < OWNERS)
        def _(q=q):
            sum_copy(q).wait_recv()

    for h in range(2):
        for r in range(7):
            for e in range(2):
                spread[pl.ds(r * 32 + h * 2 + e, 8, stride=4), :] = full[h * 7 + r, :, e * 128 : (e + 1) * 128]
    factor, step = camera_solve(lambda c: spread[4 * c : 4 * c + 4, :])
    for n, v in enumerate(step):
        steps[mine, 4 * n : 4 * n + 4, :] = v
    steps[mine, 36:40, :] = jnp.zeros((4, 128), f32)

    to_cams = []
    for d in (4, 5, 3, 2, 6, 7, 1):
        copy = pltpu.make_async_remote_copy(
            src_ref=steps.at[mine], dst_ref=steps.at[mine],
            send_sem=send_e.at[d], recv_sem=recv_e.at[d],
            device_id=(img, (mine + d) % 8), device_id_type=MESH,
        )
        copy.start()
        to_cams.append(copy)

    for n, v in enumerate(factor):
        for q in range(4):
            fac_out[n : n + 1, q * 128 : (q + 1) * 128] = v[q : q + 1]

    for d in range(4):
        core_copy(d).wait_send()
        for q in PLANE:
            if ORDER[d] or q != (0, 0):
                @pl.when(plane(q) < OWNERS)
                def _(d=d, q=q):
                    slice_copy(d, q).wait_send()

    @pl.when(img < OWNERS)
    def _():
        for q in PLANE[:15]:
            sum_copy(q).wait_send()

    for copy in to_cams:
        copy.wait_recv()
    for copy in to_cams:
        copy.wait_send()


def camera_update(jac_cam, jac_point, residual, count, cam):
    hbm = pl.BlockSpec(memory_space=pltpu.MemorySpace.HBM)
    vmem = pl.BlockSpec(memory_space=pltpu.MemorySpace.VMEM)
    dma = pltpu.SemaphoreType.DMA
    return pl.pallas_call(
        camera_kernel,
        out_shape=(
            jax.ShapeDtypeStruct((PACKED, 512), f32),
            jax.ShapeDtypeStruct((8, 40, 128), f32),
            jax.ShapeDtypeStruct((256, NOBS), bf16),
            jax.ShapeDtypeStruct((NB, 27, 8, 128), f32),
            jax.ShapeDtypeStruct((NB, 16, 128), f32),
            jax.ShapeDtypeStruct((1, NOBS), jnp.int32),
        ),
        in_specs=[hbm] * 5,
        out_specs=(vmem,) * 6,
        scratch_shapes=[
            pltpu.VMEM((NL, CP, K, 128), f32),
            pltpu.VMEM((NL, 3, K, 128), f32),
            pltpu.VMEM((NL, K, 128), f32),
            pltpu.VMEM((3, NB * K, 128, 128), f32),
            pltpu.VMEM((10, 128, 128), f32),
            pltpu.VMEM((10, 128, 128), f32),
            pltpu.VMEM((len(PAIRS), 64, 128), f32),
            pltpu.VMEM((NB, 128), jnp.int32),
            pltpu.VMEM((K, NL), jnp.int32),
            pltpu.SemaphoreType.DMA((NB + 1, 3)),
            pltpu.VMEM((2 * ROWS, NOBS), bf16),
            pltpu.VMEM((ROWS * 8, 128), f32),
            pltpu.VMEM((256, NOBS), bf16),
            pltpu.VMEM((448, NOBS), bf16),
            pltpu.VMEM((4, 16, 8, 256), f32),
            pltpu.VMEM((4, 16, 8, 256), f32),
            pltpu.VMEM((4, 16, 8, 256), f32),
            pltpu.VMEM((64, 8, 256), f32),
            pltpu.VMEM((NIMG, 8, 256), f32),
            pltpu.VMEM((ROWS * 4, 128), f32),
            dma((4,)), dma((4,)), dma((64,)), dma((64,)), dma((NIMG,)), dma((NIMG,)), dma((8,)), dma((8,)),
        ],
        compiler_params=pltpu.CompilerParams(
            collective_id=0, has_side_effects=True, vmem_limit_bytes=50 << 20
        ),
        name="marginalize_and_sum",
    )(jac_cam, jac_point, residual, count, cam)


def point_kernel(fac, steps, pick, cam, coup, small, fac_out, step_out, point_out, picked, groups):
    mine = lax.axis_index("cam")
    fac_out[...] = fac[...]
    for c in range(CP):
        for q in range(4):
            step_out[c : c + 1, q * 128 : (q + 1) * 128] = steps[mine, 4 * c + q : 4 * c + q + 1, :]
    table = steps[...].reshape(320, 128)
    high = table.astype(bf16).astype(f32)
    table = jnp.concatenate([high, table - high], axis=1).astype(bf16)
    quarter = lax.broadcasted_iota(jnp.int32, (40, 256), 0) & 3
    for b in range(NB):
        for q in range(4):
            cols = slice(b * 1024 + q * 256, b * 1024 + (q + 1) * 256)
            chosen = jnp.dot(table, pick[:, cols], preferred_element_type=f32)
            place = (cam[0:1, cols] >> 7) - quarter
            total = jnp.zeros((40, 256), f32)
            for g in range(8):
                total = total + jnp.where(place == 4 * g, chosen[40 * g : 40 * g + 40], 0.0)
            for e in range(2):
                groups[q * 2 + e] = total[:, e * 128 : (e + 1) * 128]
        for k in range(K):
            total = groups[k, pl.ds(0, 10, stride=4), :]
            for q in range(1, 4):
                total = total + groups[k, pl.ds(q, 10, stride=4), :]
            picked[pl.ds(k, 10, stride=8), :] = total
        sums = []
        for p in range(3):
            v = coup[b, p * CP] * picked[0:8, :]
            for c in range(1, CP):
                v = v + coup[b, p * CP + c] * picked[c * 8 : c * 8 + 8, :]
            sums.append(small[b, 6 + p : 7 + p, :] + jnp.sum(v, axis=0, keepdims=True))
        inv = [small[b, p : p + 1, :] for p in range(3)]
        r01, r02, r12 = [small[b, p : p + 1, :] for p in range(3, 6)]
        two = sums[2] * inv[2]
        one = (sums[1] - r12 * two) * inv[1]
        zero = (sums[0] - r01 * one - r02 * two) * inv[0]
        for p, v in enumerate((zero, one, two)):
            point_out[p : p + 1, b * 128 : (b + 1) * 128] = -v


def point_update(fac, steps, pick, cam, coup, small):
    vmem = pl.BlockSpec(memory_space=pltpu.MemorySpace.VMEM)
    return pl.pallas_call(
        point_kernel,
        out_shape=(
            jax.ShapeDtypeStruct((PACKED, 512), f32),
            jax.ShapeDtypeStruct((CP, 512), f32),
            jax.ShapeDtypeStruct((3, NL), f32),
        ),
        in_specs=[vmem] * 6,
        out_specs=(vmem,) * 3,
        scratch_shapes=[pltpu.VMEM((80, 128), f32), pltpu.VMEM((K, 40, 128), f32)],
        compiler_params=pltpu.CompilerParams(vmem_limit_bytes=32 << 20),
        name="point_update",
    )(fac, steps, pick, cam, coup, small)


def local(jac_cam, jac_point, residual, obs_count, obs_camera):
    operands = (
        jnp.transpose(jac_cam, (0, 2, 1, 3)),
        jnp.transpose(jac_point, (0, 2, 1, 3)),
        residual,
        obs_count.reshape(NB, 128),
        jnp.transpose(obs_camera),
    )
    operands = [pltpu.with_memory_space_constraint(v, pltpu.MemorySpace.HBM) for v in operands]
    fac, steps, pick, coup, small, cam = camera_update(*operands)
    return point_update(fac, steps, pick, cam, coup, small)


def solution(mesh):
    in_specs = (
        P(("img", "cam"), None, None, None),
        P(("img", "cam"), None, None, None),
        P(("img", "cam"), None, None),
        P(("img", "cam")),
        P(("img", "cam"), None),
    )
    out_specs = (P(None, "cam"), P(None, "cam"), P(None, ("img", "cam")))
    return jax.shard_map(local, mesh=mesh, in_specs=in_specs, out_specs=out_specs, check_vma=False)
```

```python
import functools

import jax
import jax.numpy as jnp
from jax import lax
from jax.experimental import pallas as pl
from jax.experimental.pallas import tpu as pltpu
from jax.sharding import PartitionSpec as P

CP = 9
K = 8
NL = 384
NB = 3
NOBS = NL * K
PACKED = 45
ROWS = 56
NIMG = 16
LM_LAMBDA = 0.5
f32 = jnp.float32
bf16 = jnp.bfloat16
MESH = pl.DeviceIdType.MESH

CC = [(i, j) for i in range(CP) for j in range(i, CP)]
CR = [(i, 9) for i in range(CP)]
QC = [(10 + p, c) for p in range(3) for c in range(CP)]
QR = [(10 + p, 9) for p in range(3)]
PAIRS = CC + CR + QC + QR
GROUPS = [PAIRS[0:28], PAIRS[28:56], PAIRS[56:84]]


def pair_positions():
    position = {}
    for i in range(CP):
        for j in range(i, CP):
            position[i, j] = len(position)
    return position


def camera_solve(load):
    position = pair_positions()
    factor, inverse = {}, []
    for j in range(CP):
        for i in range(j, CP):
            amount = load(position[j, i])
            if i == j:
                amount = amount + LM_LAMBDA
            for k in range(j):
                amount = amount - factor[k, j] * factor[k, i]
            if i == j:
                factor[j, j] = jnp.sqrt(amount)
                inverse.append(1.0 / factor[j, j])
            else:
                factor[j, i] = amount * inverse[j]
    forward = []
    for j in range(CP):
        amount = load(PACKED + j)
        for k in range(j):
            amount = amount - factor[k, j] * forward[k]
        forward.append(amount * inverse[j])
    backward = [None] * CP
    for i in range(CP - 1, -1, -1):
        amount = forward[i]
        for j in range(i + 1, CP):
            amount = amount - factor[i, j] * backward[j]
        backward[i] = amount * inverse[i]
    return [factor[i, j] for i in range(CP) for j in range(i, CP)], [-v for v in backward]


def fill_onehot(cam, onehot):
    for t in range(NOBS // 256):
        lane = cam[0:1, t * 256 : (t + 1) * 256] & 255
        hit = lax.broadcasted_iota(jnp.int32, (256, 256), 0) == lane
        onehot[:, t * 256 : (t + 1) * 256] = hit.astype(f32).astype(bf16)


PLANE = sorted(((a, b) for a in range(4) for b in range(4)), key=lambda q: -min(q[0], 4 - q[0]) - min(q[1], 4 - q[1]))
OWNERS = 14


def camera_kernel(
    jc, jp, rs, cnt_hbm, cam_hbm, fac_out, steps, pick, coup_out, small_out, cam_out,
    jcv, jpv, rsv, qt, ta, tb, acc, cnt, cam, sem,
    rec, turned, onehot, lhs, away, home, from_core, arrived, full, spread,
    send_a, recv_a, send_c, recv_c, send_d, recv_d, send_e, recv_e,
):
    img, mine = lax.axis_index("img"), lax.axis_index("cam")
    z, x, y, core = img // 4, img % 4, mine // 2, mine % 2

    def plane(q):
        return ((z + q[0]) % 4) * 4 + (x + q[1]) % 4

    barrier = pltpu.get_barrier_semaphore()
    pl.semaphore_signal(barrier, inc=1, device_id=(img, y * 2 + 1 - core), device_id_type=MESH)
    for dy in range(4):
        for q in PLANE:
            if dy or q != (0, 0):
                pl.semaphore_signal(
                    barrier, inc=1, device_id=(plane(q), ((y + dy) % 4) * 2 + core), device_id_type=MESH
                )
    for dy in range(1, 4):
        pl.semaphore_signal(
            barrier, inc=1, device_id=(img, ((y + dy) % 4) * 2 + 1 - core), device_id_type=MESH
        )

    def copy(b, which):
        s = pl.ds(b * 128, 128)
        src, dst = ((jp, jpv), (jc, jcv), (rs, rsv))[which]
        return pltpu.make_async_copy(src.at[s], dst.at[s], sem.at[b, which])

    count_copy = pltpu.make_async_copy(cnt_hbm, cnt, sem.at[NB, 0])
    cam_copy = pltpu.make_async_copy(cam_hbm, cam, sem.at[NB, 1])
    count_copy.start()
    cam_copy.start()
    for which in range(3):
        for b in range(NB):
            copy(b, which).start()
    count_copy.wait()
    cam_copy.wait()
    for b in range(NB):
        for k in range(K):
            cam_out[0:1, (b * K + k) * 128 : (b * K + k + 1) * 128] = cam[k : k + 1, b * 128 : (b + 1) * 128]
    fill_onehot(cam_out, onehot)

    jcf = jcv.reshape(NL * CP * K, 128)
    jpf = jpv.reshape(NL * 3 * K, 128)
    rsf = rsv.reshape(NL * K, 128)

    def point_phase(b, _):
        copy(b, 0).wait()
        count = cnt[pl.ds(b, 1), :]
        zero = jnp.zeros((8, 128), f32)

        def first(k, sums):
            live = (count > k).astype(f32)
            parts = []
            for p in range(3):
                v = jpf[pl.ds(b * (128 * 3 * K) + p * K + k, 128, stride=3 * K), :].T * live
                qt[p, b * K + k] = v
                parts.append(v)
            sums = list(sums)
            for x in range(16):
                a = [v[8 * x : 8 * x + 8] for v in parts]
                for q in range(3):
                    sums[q] = sums[q] + a[0] * a[q]
            return tuple(sums)

        s00, s01, s02 = [
            jnp.sum(v, axis=0, keepdims=True) for v in lax.fori_loop(0, K, first, (zero,) * 3, unroll=K)
        ]
        norm0 = jnp.sqrt(s00)
        inv0 = 1.0 / norm0
        r01 = s01 * inv0
        r02 = s02 * inv0
        c01 = r01 * inv0
        c02 = r02 * inv0

        def second(k, sums):
            n1, s12 = sums
            for x in range(16):
                rows = pl.ds(8 * x, 8)
                rem = qt[1, b * K + k, rows, :] - c01 * qt[0, b * K + k, rows, :]
                qt[1, b * K + k, rows, :] = rem
                n1 = n1 + rem * rem
                s12 = s12 + rem * qt[2, b * K + k, rows, :]
            return n1, s12

        n11, s12 = [
            jnp.sum(v, axis=0, keepdims=True) for v in lax.fori_loop(0, K, second, (zero,) * 2, unroll=K)
        ]
        norm1 = jnp.sqrt(n11)
        inv1 = 1.0 / norm1
        r12 = s12 * inv1
        c12 = r12 * inv1

        def third(k, n2):
            for x in range(16):
                rows = pl.ds(8 * x, 8)
                rem = (
                    qt[2, b * K + k, rows, :]
                    - c02 * qt[0, b * K + k, rows, :]
                    - c12 * qt[1, b * K + k, rows, :]
                )
                qt[2, b * K + k, rows, :] = rem
                n2 = n2 + rem * rem
            return n2

        n22 = jnp.sum(lax.fori_loop(0, K, third, zero, unroll=K), axis=0, keepdims=True)
        norm2 = jnp.sqrt(n22)
        inv2 = 1.0 / norm2
        for n, v in enumerate((inv0, inv1, inv2, r01, r02, r12)):
            small_out[b, n : n + 1, :] = v
        return 0

    lax.fori_loop(0, NB, point_phase, 0)

    def turn(b, k, t):
        for c in range(CP):
            t[c] = jcf[pl.ds(b * (128 * CP * K) + c * K + k, 128, stride=CP * K), :].T
        t[9] = rsf[pl.ds(b * (128 * K) + k, 128, stride=K), :].T

    def products(b, k, t):
        base = 0
        for pairs in GROUPS:
            total = [None] * len(pairs)
            for x in range(16):
                rows = pl.ds(8 * x, 8)
                held = {}
                for n, pair in enumerate(pairs):
                    for q in pair:
                        if q not in held:
                            held[q] = t[q, rows, :] if q < 10 else qt[q - 10, b * K + k, rows, :]
                    term = held[pair[0]] * held[pair[1]]
                    total[n] = term if total[n] is None else total[n] + term
            for n in range(len(pairs)):
                acc[base + n, 8 * k : 8 * k + 8, :] = total[n]
            base += len(pairs)

    def camera_phase(b, _):
        copy(b, 1).wait()
        copy(b, 2).wait()
        turn(b, 0, ta)

        for k in range(K):
            now, later = (ta, tb) if k % 2 == 0 else (tb, ta)
            if k + 1 < K:
                turn(b, k + 1, later)
            products(b, k, now)

        def entry(n):
            v = acc[n, pl.ds(0, 8, stride=8), :]
            for s in range(1, 8):
                v = v + acc[n, pl.ds(s, 8, stride=8), :]
            return v

        slot = lax.broadcasted_iota(jnp.int32, (8, 128), 0)
        live = (slot < cnt[pl.ds(b, 1), :]).astype(f32)
        inv = [small_out[b, p : p + 1, :] for p in range(3)]
        coupling = [[entry(54 + p * CP + c) * inv[p] for c in range(CP)] for p in range(3)]
        for p in range(3):
            for c in range(CP):
                coup_out[b, p * CP + c] = coupling[p][c]
        rhs = [jnp.sum(entry(81 + p), axis=0, keepdims=True) * inv[p] for p in range(3)]
        for p in range(3):
            small_out[b, 6 + p : 7 + p, :] = rhs[p]
        for n, (i, j) in enumerate(CC):
            v = entry(n) * live
            for p in range(3):
                v = v - coupling[p][i] * coupling[p][j]
            turned[n * 8 : n * 8 + 8, :] = v
        for i in range(CP):
            v = entry(45 + i) * live
            for p in range(3):
                v = v - coupling[p][i] * rhs[p]
            turned[(45 + i) * 8 : (45 + i) * 8 + 8, :] = v
        for i in range(54, ROWS):
            turned[i * 8 : i * 8 + 8, :] = jnp.zeros((8, 128), f32)
        for k in range(K):
            v = turned[pl.ds(k, ROWS, stride=8), :]
            high = v.astype(bf16).astype(f32)
            both = jnp.concatenate([high, v - high], axis=0).astype(bf16)
            rec[:, pl.ds(pl.multiple_of((b * K + k) * 128, 128), 128)] = both
        return 0

    lax.fori_loop(0, NB, camera_phase, 0)

    def sums_of(owners):
        for n, owner in enumerate(owners):
            for half in range(2):
                rows = slice((n * 2 + half) * 112, (n * 2 + half + 1) * 112)
                for t in range(6):
                    cols = slice(t * 512, (t + 1) * 512)
                    hit = (cam_out[0:1, cols] >> 8) == owner * 2 + half
                    mask = jnp.broadcast_to(hit.astype(f32), (16, 512)).astype(bf16)
                    mask = jnp.concatenate([mask] * 7, axis=0)
                    lhs[rows, cols] = rec[:, cols] * mask
        r = lax.dot_general(
            lhs[...], onehot[...], (((1,), (1,)), ((), ())), preferred_element_type=f32
        )
        return [r[112 * h : 112 * h + 56] + r[112 * h + 56 : 112 * h + 112] for h in range(4)]

    ORDER = (2, 1, 3, 0)

    def core_copy(d):
        return pltpu.make_async_remote_copy(
            src_ref=away.at[d, pl.ds(0, OWNERS)], dst_ref=from_core.at[d, pl.ds(0, OWNERS)],
            send_sem=send_a.at[d], recv_sem=recv_a.at[d],
            device_id=(img, y * 2 + 1 - core), device_id_type=MESH,
        )

    def both_cores(d):
        to_y = (y + ORDER[d]) % 4
        sums = sums_of((to_y * 2 + 1 - core, to_y * 2 + core))
        for h in range(2):
            for r in range(7):
                away[d, h * 7 + r] = sums[h][8 * r : 8 * r + 8]
                home[d, h * 7 + r] = sums[2 + h][8 * r : 8 * r + 8]
        core_copy(d).start()

    def slice_copy(d, q):
        n = ORDER[d] * 16 + q[0] * 4 + q[1]
        return pltpu.make_async_remote_copy(
            src_ref=home.at[d, plane(q)], dst_ref=arrived.at[n],
            send_sem=send_c.at[n], recv_sem=recv_c.at[n],
            device_id=(plane(q), ((y + ORDER[d]) % 4) * 2 + core), device_id_type=MESH,
        )

    def send_on(d):
        core_copy(d).wait_recv()
        home[d, 0:OWNERS] = home[d, 0:OWNERS] + from_core[d, 0:OWNERS]
        for q in PLANE:
            if ORDER[d] or q != (0, 0):
                @pl.when(plane(q) < OWNERS)
                def _(q=q):
                    slice_copy(d, q).start()

    pl.semaphore_wait(barrier, 67)
    both_cores(0)
    for d in range(1, 4):
        both_cores(d)
        send_on(d - 1)
    send_on(3)

    def sum_copy(q):
        n = q[0] * 4 + q[1]
        return pltpu.make_async_remote_copy(
            src_ref=full.at[img], dst_ref=full.at[img],
            send_sem=send_d.at[n], recv_sem=recv_d.at[n],
            device_id=(plane(q), mine), device_id_type=MESH,
        )

    @pl.when(img < OWNERS)
    def _():
        total = home[3, img]
        for d in range(4):
            for q in PLANE:
                if ORDER[d] or q != (0, 0):
                    slice_copy(d, q).wait_recv()
                    total = total + arrived[ORDER[d] * 16 + q[0] * 4 + q[1]]
        full[img] = total
        for q in PLANE[:15]:
            sum_copy(q).start()

    for t in range(NOBS // 256):
        cols = slice(t * 256, (t + 1) * 256)
        hit = lax.broadcasted_iota(jnp.int32, (128, 256), 0) == (cam_out[0:1, cols] & 127)
        hit = hit.astype(f32).astype(bf16)
        pick[0:128, cols] = hit
        pick[128:256, cols] = hit

    for q in PLANE[:15]:
        @pl.when(plane(((4 - q[0]) % 4, (4 - q[1]) % 4)) < OWNERS)
        def _(q=q):
            sum_copy(q).wait_recv()

    for h in range(2):
        for r in range(7):
            for e in range(2):
                spread[pl.ds(r * 32 + h * 2 + e, 8, stride=4), :] = full[h * 7 + r, :, e * 128 : (e + 1) * 128]
    factor, step = camera_solve(lambda c: spread[4 * c : 4 * c + 4, :])
    for n, v in enumerate(step):
        steps[mine, 4 * n : 4 * n + 4, :] = v
    steps[mine, 36:40, :] = jnp.zeros((4, 128), f32)

    to_cams = []
    for d in (4, 5, 3, 2, 6, 7, 1):
        copy = pltpu.make_async_remote_copy(
            src_ref=steps.at[mine], dst_ref=steps.at[mine],
            send_sem=send_e.at[d], recv_sem=recv_e.at[d],
            device_id=(img, (mine + d) % 8), device_id_type=MESH,
        )
        copy.start()
        to_cams.append(copy)

    for n, v in enumerate(factor):
        for q in range(4):
            fac_out[n : n + 1, q * 128 : (q + 1) * 128] = v[q : q + 1]

    for d in range(4):
        core_copy(d).wait_send()
        for q in PLANE:
            if ORDER[d] or q != (0, 0):
                @pl.when(plane(q) < OWNERS)
                def _(d=d, q=q):
                    slice_copy(d, q).wait_send()

    @pl.when(img < OWNERS)
    def _():
        for q in PLANE[:15]:
            sum_copy(q).wait_send()

    for copy in to_cams:
        copy.wait_recv()
    for copy in to_cams:
        copy.wait_send()


def camera_update(jac_cam, jac_point, residual, count, cam):
    hbm = pl.BlockSpec(memory_space=pltpu.MemorySpace.HBM)
    vmem = pl.BlockSpec(memory_space=pltpu.MemorySpace.VMEM)
    dma = pltpu.SemaphoreType.DMA
    return pl.pallas_call(
        camera_kernel,
        out_shape=(
            jax.ShapeDtypeStruct((PACKED, 512), f32),
            jax.ShapeDtypeStruct((8, 40, 128), f32),
            jax.ShapeDtypeStruct((256, NOBS), bf16),
            jax.ShapeDtypeStruct((NB, 27, 8, 128), f32),
            jax.ShapeDtypeStruct((NB, 16, 128), f32),
            jax.ShapeDtypeStruct((1, NOBS), jnp.int32),
        ),
        in_specs=[hbm] * 5,
        out_specs=(vmem,) * 6,
        scratch_shapes=[
            pltpu.VMEM((NL, CP, K, 128), f32),
            pltpu.VMEM((NL, 3, K, 128), f32),
            pltpu.VMEM((NL, K, 128), f32),
            pltpu.VMEM((3, NB * K, 128, 128), f32),
            pltpu.VMEM((10, 128, 128), f32),
            pltpu.VMEM((10, 128, 128), f32),
            pltpu.VMEM((len(PAIRS), 64, 128), f32),
            pltpu.VMEM((NB, 128), jnp.int32),
            pltpu.VMEM((K, NL), jnp.int32),
            pltpu.SemaphoreType.DMA((NB + 1, 3)),
            pltpu.VMEM((2 * ROWS, NOBS), bf16),
            pltpu.VMEM((ROWS * 8, 128), f32),
            pltpu.VMEM((256, NOBS), bf16),
            pltpu.VMEM((448, NOBS), bf16),
            pltpu.VMEM((4, 16, 8, 256), f32),
            pltpu.VMEM((4, 16, 8, 256), f32),
            pltpu.VMEM((4, 16, 8, 256), f32),
            pltpu.VMEM((64, 8, 256), f32),
            pltpu.VMEM((NIMG, 8, 256), f32),
            pltpu.VMEM((ROWS * 4, 128), f32),
            dma((4,)), dma((4,)), dma((64,)), dma((64,)), dma((NIMG,)), dma((NIMG,)), dma((8,)), dma((8,)),
        ],
        compiler_params=pltpu.CompilerParams(
            collective_id=0, has_side_effects=True, vmem_limit_bytes=50 << 20
        ),
        name="marginalize_and_sum",
    )(jac_cam, jac_point, residual, count, cam)


def point_kernel(fac, steps, pick, cam, coup, small, fac_out, step_out, point_out, picked, groups):
    mine = lax.axis_index("cam")
    fac_out[...] = fac[...]
    for c in range(CP):
        for q in range(4):
            step_out[c : c + 1, q * 128 : (q + 1) * 128] = steps[mine, 4 * c + q : 4 * c + q + 1, :]
    table = steps[...].reshape(320, 128)
    high = table.astype(bf16).astype(f32)
    table = jnp.concatenate([high, table - high], axis=1).astype(bf16)
    quarter = lax.broadcasted_iota(jnp.int32, (40, 256), 0) & 3
    for b in range(NB):
        for q in range(4):
            cols = slice(b * 1024 + q * 256, b * 1024 + (q + 1) * 256)
            chosen = jnp.dot(table, pick[:, cols], preferred_element_type=f32)
            place = (cam[0:1, cols] >> 7) - quarter
            total = jnp.zeros((40, 256), f32)
            for g in range(8):
                total = total + jnp.where(place == 4 * g, chosen[40 * g : 40 * g + 40], 0.0)
            for e in range(2):
                groups[q * 2 + e] = total[:, e * 128 : (e + 1) * 128]
        for k in range(K):
            total = groups[k, pl.ds(0, 10, stride=4), :]
            for q in range(1, 4):
                total = total + groups[k, pl.ds(q, 10, stride=4), :]
            picked[pl.ds(k, 10, stride=8), :] = total
        sums = []
        for p in range(3):
            v = coup[b, p * CP] * picked[0:8, :]
            for c in range(1, CP):
                v = v + coup[b, p * CP + c] * picked[c * 8 : c * 8 + 8, :]
            sums.append(small[b, 6 + p : 7 + p, :] + jnp.sum(v, axis=0, keepdims=True))
        inv = [small[b, p : p + 1, :] for p in range(3)]
        r01, r02, r12 = [small[b, p : p + 1, :] for p in range(3, 6)]
        two = sums[2] * inv[2]
        one = (sums[1] - r12 * two) * inv[1]
        zero = (sums[0] - r01 * one - r02 * two) * inv[0]
        for p, v in enumerate((zero, one, two)):
            point_out[p : p + 1, b * 128 : (b + 1) * 128] = -v


def point_update(fac, steps, pick, cam, coup, small):
    vmem = pl.BlockSpec(memory_space=pltpu.MemorySpace.VMEM)
    return pl.pallas_call(
        point_kernel,
        out_shape=(
            jax.ShapeDtypeStruct((PACKED, 512), f32),
            jax.ShapeDtypeStruct((CP, 512), f32),
            jax.ShapeDtypeStruct((3, NL), f32),
        ),
        in_specs=[vmem] * 6,
        out_specs=(vmem,) * 3,
        scratch_shapes=[pltpu.VMEM((80, 128), f32), pltpu.VMEM((K, 40, 128), f32)],
        compiler_params=pltpu.CompilerParams(vmem_limit_bytes=32 << 20),
        name="point_update",
    )(fac, steps, pick, cam, coup, small)


def local(jac_cam, jac_point, residual, obs_count, obs_camera):
    operands = (
        jnp.transpose(jac_cam, (0, 2, 1, 3)),
        jnp.transpose(jac_point, (0, 2, 1, 3)),
        residual,
        obs_count.reshape(NB, 128),
        jnp.transpose(obs_camera),
    )
    operands = [pltpu.with_memory_space_constraint(v, pltpu.MemorySpace.HBM) for v in operands]
    fac, steps, pick, coup, small, cam = camera_update(*operands)
    return point_update(fac, steps, pick, cam, coup, small)


def solution(mesh):
    in_specs = (
        P(("img", "cam"), None, None, None),
        P(("img", "cam"), None, None, None),
        P(("img", "cam"), None, None),
        P(("img", "cam")),
        P(("img", "cam"), None),
    )
    out_specs = (P(None, "cam"), P(None, "cam"), P(None, ("img", "cam")))
    return jax.shard_map(local, mesh=mesh, in_specs=in_specs, out_specs=out_specs, check_vma=False)
```
